32 devices in a mesh: seq: 8 (over z, x), ch: 4 (over y, core).
Axes of the slice: x: 2, y: 2, z: 4, core: 2. Of those that a mesh axis runs over, the one named last changes fastest.
Arguments:
- inputs: float32 [2048, 4096], P('seq', 'ch'), may hold values from -6 to 6
- out_grads: float32 [2048, 4096], P('seq', 'ch'), may hold values from -0.12 to 0.12
- tile_order: int32 [8], replicated, may hold values from 0 to 7, each once
- lag_order: int32 [8], replicated, may hold values from 0 to 7, each once
Outputs:
- filter_grad: float32 [256, 2048], P('ch', 'seq')
The draws below stay inside these ranges and needn't reach their ends.
Inputs may be any that keep to these rules, and one draw needn't show every extreme that they name: Row block i of inputs and out_grads holds sequence tile tile_order[i]; every tile appears once. Column block i of filter_grad holds lag block lag_order[i]; every lag block appears once.
All inputs are finite; a program needn't handle non-finite values.
Results may differ from the reference program's by a relative error of at most 0.000098.
Values sent between devices are 32-bit elements; how exact they have to be, the bound alone decides.
No kernel may reach another device: no remote copies, remote signals or barrier semaphores. Data moves between devices by JAX's collectives and lax.ppermute only.
A program may use at most 128 MiB of HBM per device.

```python
import jax
import jax.numpy as jnp

TOK_DEV = 256
C = 4096
GROUP = 16
TOKENS = 2048
N_SEQ = 8


def steps_of(rng, extent, cuts, low, top_value):
    level, own = 1.0, jax.random.fold_in(rng, 6)
    for dim, blocks in cuts:
        heights = jnp.exp(jax.random.uniform(jax.random.fold_in(own, dim), (blocks,), jnp.float32, low / len(cuts), top_value / len(cuts)))
        level = level * jnp.repeat(heights, extent[dim] // blocks).reshape([-1 if axis == dim else 1 for axis in range(len(extent))])
    return level


def normal_values(rng, extent, scale, reach, pieces=(), kind=jnp.bfloat16):
    drawn = jax.random.normal(rng, extent, jnp.float32) * scale
    if len(pieces) > 0:
        drawn = steps_of(rng, extent, pieces, -0.22, 0.18) * drawn
    return jnp.clip(drawn, min=-reach, max=reach).astype(kind)


def setup_inputs(seed: int = 0) -> dict:
    streams_of = jax.random.split(jax.random.key(seed), 5)
    return {
        "inputs": normal_values(streams_of[0], (TOKENS, C), 1.0, 6.0, ((0, 8), (1, 4)), jnp.float32),
        "out_grads": normal_values(streams_of[1], (TOKENS, C), 0.02, 0.12, ((0, 8), (1, 4)), jnp.float32),
        "tile_order": jax.random.permutation(streams_of[2], N_SEQ).astype(jnp.int32),
        "lag_order": jax.random.permutation(streams_of[3], N_SEQ).astype(jnp.int32),
    }


target_ratio = 0.5
epsilon = 1e-12

def reference(inputs, out_grads, tile_order, lag_order):
    blocks = N_SEQ
    channels = inputs.shape[1]
    length = blocks * TOK_DEV
    natural_inputs = jnp.zeros((blocks, TOK_DEV, channels), jnp.float32).at[tile_order].set(inputs.reshape(blocks, TOK_DEV, channels)).reshape(length, channels)
    natural_grads = jnp.zeros((blocks, TOK_DEV, channels), jnp.float32).at[tile_order].set(out_grads.reshape(blocks, TOK_DEV, channels)).reshape(length, channels)
    input_spectrum = jnp.fft.rfft(natural_inputs, n=2 * length, axis=0)
    grad_spectrum = jnp.fft.rfft(natural_grads, n=2 * length, axis=0)
    correlation = jnp.fft.irfft(jnp.conj(input_spectrum) * grad_spectrum, n=2 * length, axis=0)[:length]
    grouped = correlation.reshape(length, channels // GROUP, GROUP).sum(axis=2).T
    squares = jnp.sum(grouped * grouped)
    factor = target_ratio * grouped.size ** 0.5 / jnp.sqrt(squares + epsilon)
    scaled = grouped * factor
    owned_blocks = scaled.reshape(channels // GROUP, blocks, TOK_DEV)[:, lag_order].reshape(channels // GROUP, length)
    return owned_blocks
```

```python
import functools
import math

import jax
import jax.numpy as jnp
import ml_dtypes
import numpy as np
from jax import lax
from jax.experimental import pallas as pl
from jax.experimental.pallas import tpu as pltpu
from jax.sharding import PartitionSpec as P

GROUP = 16
target_ratio = 0.5
epsilon = 1e-12


def halves(table):
    high = table.astype(ml_dtypes.bfloat16)
    low = (table - high.astype(np.float64)).astype(ml_dtypes.bfloat16)
    return high, low


def forward_table(rows):
    angles = np.outer(2 * np.arange(rows) + 1, np.arange(rows)) % (4 * rows) * (math.pi / (2 * rows))
    high, low = halves(np.concatenate([np.cos(angles), -np.sin(angles)], axis=0))
    return np.concatenate([high, low, high], axis=1)


def inverse_table(rows):
    angles = np.outer(2 * np.arange(rows) + 1, np.arange(2 * rows)) % (4 * rows) * (math.pi / (2 * rows))
    sign = np.where(np.arange(2 * rows) < rows, 1.0, -1.0) / rows
    high, low = halves(np.concatenate([np.cos(angles) * sign, -np.sin(angles) * sign], axis=0))
    return np.concatenate([high, high, low], axis=0)


def group_table(tiles, channels):
    columns = np.arange(tiles * channels)
    return (columns[:, None] // GROUP == np.arange(tiles * channels // GROUP)[None, :]).astype(ml_dtypes.bfloat16)


def split(values):
    high = values.astype(jnp.bfloat16)
    low = (values - high.astype(jnp.float32)).astype(jnp.bfloat16)
    return high, low


def lag_kernel(tiles, channels, rows, tile_ref, lag_ref, forward_ref, inverse_ref, group_ref, *refs):
    blocks, (out_ref, spectra, products, natural) = refs[:tiles], refs[tiles:]
    groups = channels // GROUP
    for slot in range(tiles):
        high, low = split(blocks[slot][...])
        spectra[tile_ref[slot]] = jnp.dot(
            forward_ref[...],
            jnp.concatenate([high, high, low], axis=0),
            preferred_element_type=jnp.float32,
        )

    def row_step(step, carry):
        real = pl.ds(pl.multiple_of(step * 8, 8), 8)
        imag = pl.ds(pl.multiple_of(rows + step * 8, 8), 8)
        input_real = [spectra[tile, real, :channels] for tile in range(tiles)]
        input_imag = [spectra[tile, imag, :channels] for tile in range(tiles)]
        grad_real = [spectra[tile, real, channels:] for tile in range(tiles)]
        grad_imag = [spectra[tile, imag, channels:] for tile in range(tiles)]
        for offset in range(tiles):
            total_real = total_imag = None
            for tile in range(tiles - offset):
                first, second = (input_real[tile], input_imag[tile]), (grad_real[tile + offset], grad_imag[tile + offset])
                term_real = first[0] * second[0] + first[1] * second[1]
                term_imag = first[0] * second[1] - first[1] * second[0]
                total_real = term_real if total_real is None else total_real + term_real
                total_imag = term_imag if total_imag is None else total_imag + term_imag
            columns = slice(offset * channels, (offset + 1) * channels)
            products[real, columns] = total_real
            products[imag, columns] = total_imag
        return carry

    lax.fori_loop(0, rows // 8, row_step, 0)
    high, low = split(products[...])
    grouped = jnp.dot(high, group_ref[...], preferred_element_type=jnp.float32)
    grouped = grouped + jnp.dot(low, group_ref[...], preferred_element_type=jnp.float32)
    high, low = split(grouped.T)
    circular = jnp.dot(
        jnp.concatenate([high, low, high], axis=1), inverse_ref[...], preferred_element_type=jnp.float32
    )
    following = jnp.concatenate([circular[groups:, rows:], jnp.zeros((groups, rows), jnp.float32)], axis=0)
    lags = circular[:, :rows] + following
    squares = jnp.broadcast_to(jnp.sum(lags * lags, keepdims=True), (8, rows))
    for offset in range(tiles):
        natural[offset] = lags[offset * groups : (offset + 1) * groups]
    for slot in range(tiles):
        out_ref[slot, :groups, :] = natural[lag_ref[slot]]
        out_ref[slot, groups:, :] = squares


def lag_values(blocks, block_tiles, lag_order):
    tiles = len(blocks)
    rows, channels = blocks[0].shape[0], blocks[0].shape[1] // 2
    groups = channels // GROUP
    vmem = pl.BlockSpec(memory_space=pltpu.VMEM)
    smem = pl.BlockSpec(memory_space=pltpu.SMEM)
    return pl.pallas_call(
        functools.partial(lag_kernel, tiles, channels, rows),
        out_shape=jax.ShapeDtypeStruct((tiles, groups + 8, rows), jnp.float32),
        in_specs=[smem, smem] + [vmem] * (3 + tiles),
        out_specs=vmem,
        scratch_shapes=[
            pltpu.VMEM((tiles, 2 * rows, 2 * channels), jnp.float32),
            pltpu.VMEM((2 * rows, tiles * channels), jnp.float32),
            pltpu.VMEM((tiles, groups, rows), jnp.float32),
        ],
        compiler_params=pltpu.CompilerParams(vmem_limit_bytes=48 * 2**20),
        cost_estimate=pl.CostEstimate(
            flops=12 * tiles * rows * rows * channels, bytes_accessed=tiles * rows * channels * 8, transcendentals=0
        ),
    )(
        block_tiles,
        lag_order,
        jnp.asarray(forward_table(rows)),
        jnp.asarray(inverse_table(rows)),
        jnp.asarray(group_table(tiles, channels)),
        *blocks,
    )


def exchanges(count, place):
    if count & (count - 1) == 0:
        return [([(here, here ^ step) for here in range(count)], place ^ step, place ^ step) for step in range(count)]
    return [
        ([(here, (here + step) % count) for here in range(count)], (place + step) % count, (place - step) % count)
        for step in range(count)
    ]


def shards(inputs, out_grads, tile_order, lag_order):
    count = lax.axis_size("seq")
    rows = inputs.shape[0]
    channels = inputs.shape[1] // count
    blocks, sources = [], []
    for step, (pairs, target, source) in enumerate(exchanges(count, lax.axis_index("seq"))):
        block = jnp.concatenate(
            [
                lax.dynamic_slice_in_dim(inputs, target * channels, channels, 1),
                lax.dynamic_slice_in_dim(out_grads, target * channels, channels, 1),
            ],
            axis=1,
        )
        blocks.append(lax.ppermute(block, "seq", pairs) if step else block)
        sources.append(source)
    block_tiles = tile_order[jnp.stack(sources)]
    sent = lag_values(blocks, block_tiles, lag_order)
    groups = channels // GROUP
    owned = lax.all_to_all(sent, "seq", split_axis=0, concat_axis=0, tiled=True)
    squares = jnp.sum(owned[:, groups, :128], axis=0)
    ways = lax.axis_size("ch")
    total = squares
    for step in range(1, ways):
        total = total + lax.ppermute(squares, "ch", [(place, (place + step) % ways) for place in range(ways)])
    lags = owned[:, :groups, :].reshape(count * groups, rows)
    entries = ways * count * groups * count * rows
    factor = target_ratio * math.sqrt(entries) / jnp.sqrt(total[:1] + epsilon)
    return lags * factor


def solution(mesh):
    return jax.shard_map(
        shards,
        mesh=mesh,
        in_specs=(P("seq", "ch"), P("seq", "ch"), P(), P()),
        out_specs=P("ch", "seq"),
        check_vma=False,
    )
```

```python
import functools
import math

import jax
import jax.numpy as jnp
import ml_dtypes
import numpy as np
from jax import lax
from jax.experimental import pallas as pl
from jax.experimental.pallas import tpu as pltpu
from jax.sharding import PartitionSpec as P

GROUP = 16
target_ratio = 0.5
epsilon = 1e-12


def halves(table):
    high = table.astype(ml_dtypes.bfloat16)
    low = (table - high.astype(np.float64)).astype(ml_dtypes.bfloat16)
    return np.concatenate([high, high, low], axis=0)


def forward_table(rows):
    angles = np.outer(np.arange(rows), 2 * np.arange(rows) + 1) % (4 * rows) * (math.pi / (2 * rows))
    return halves(np.concatenate([np.cos(angles), -np.sin(angles)], axis=1))


def inverse_table(rows):
    angles = np.outer(2 * np.arange(rows) + 1, np.arange(rows)) % (4 * rows) * (math.pi / (2 * rows))
    return halves(np.concatenate([np.cos(angles), np.sin(angles)], axis=0) / rows)


def split(values):
    high = values.astype(jnp.bfloat16)
    low = (values - high.astype(jnp.float32)).astype(jnp.bfloat16)
    return jnp.concatenate([high, low, high], axis=1)


def partner(count, place, step, back=False):
    if count & (count - 1) == 0:
        return place ^ step
    return (place - step if back else place + step) % count


def cut_kernel(count, channels, steps, me_ref, inputs_ref, grads_ref, *refs):
    blocks, (held, in_sems, out_sems) = refs[:-3], refs[-3:]
    arriving, leaving = [], []
    for index, step in enumerate(steps):
        start = pl.multiple_of(partner(count, me_ref[0], step) * channels, channels)
        for half, ref in enumerate((inputs_ref, grads_ref)):
            arriving.append(
                pltpu.make_async_copy(
                    ref.at[:, pl.ds(start, channels)],
                    held.at[index, :, pl.ds(half * channels, channels)],
                    in_sems.at[2 * index + half],
                )
            )
        leaving.append(pltpu.make_async_copy(held.at[index], blocks[index], out_sems.at[index]))
    for copy in arriving:
        copy.start()
    for index, copy in enumerate(leaving):
        arriving[2 * index].wait()
        arriving[2 * index + 1].wait()
        copy.start()
    for copy in leaving:
        copy.wait()


def cut(inputs, out_grads, me, count, steps):
    rows, channels = inputs.shape[0], inputs.shape[1] // count
    if channels % 128:
        blocks = []
        for step in steps:
            start = partner(count, me[0], step) * channels
            pair = [lax.dynamic_slice_in_dim(whole, start, channels, 1) for whole in (inputs, out_grads)]
            blocks.append(jnp.concatenate(pair, axis=1))
        return blocks
    anywhere = pl.BlockSpec(memory_space=pl.ANY)
    return pl.pallas_call(
        functools.partial(cut_kernel, count, channels, steps),
        out_shape=[jax.ShapeDtypeStruct((rows, 2 * channels), jnp.float32) for _ in steps],
        in_specs=[pl.BlockSpec(memory_space=pltpu.SMEM), anywhere, anywhere],
        out_specs=[anywhere for _ in steps],
        scratch_shapes=[
            pltpu.VMEM((len(steps), rows, 2 * channels), jnp.float32),
            pltpu.SemaphoreType.DMA((2 * len(steps),)),
            pltpu.SemaphoreType.DMA((len(steps),)),
        ],
        cost_estimate=pl.CostEstimate(flops=0, bytes_accessed=len(steps) * rows * channels * 16, transcendentals=0),
    )(me, inputs, out_grads)


def absorb_kernel(count, channels, rows, new, olds, last, me_ref, order_ref, lag_ref, forward_ref, *refs):
    refs = list(refs)
    take = lambda many: [refs.pop(0) for _ in range(many)]
    inverse_ref = take(1)[0] if last else None
    blocks, spectra = take(len(new)), take(len(olds))
    carried = take(1)[0] if olds else None
    out_ref = take(1)[0]
    fresh = take(1)[0]
    sums, turned, tile_of = take(3)
    width = turned.shape[2]
    groups = channels // GROUP
    chunk = max(8, groups)

    if carried is None:
        sums[...] = jnp.zeros_like(sums)
    else:
        sums[...] = carried[...]
    for index, step in enumerate(new):
        flipped = blocks[index][...].T
        columns = []
        for part in range(rows // width):
            turned[part] = flipped[:, part * width : (part + 1) * width]
            members = [
                turned[part, pl.ds(half * channels + member, groups, stride=GROUP), :]
                for half in range(2)
                for member in range(GROUP)
            ]
            columns.append(jnp.concatenate(members, axis=0))
        fresh[index] = jnp.dot(
            split(jnp.concatenate(columns, axis=1)), forward_ref[...], preferred_element_type=jnp.float32
        )
    slots = list(new) + [step for old in olds for step in old]
    for index, step in enumerate(slots):
        tile_of[index] = order_ref[partner(count, me_ref[0], step, back=True)]

    def pair(ref, first, new_index, index):
        new_tile, tile = tile_of[new_index], tile_of[first + index]
        later = new_tile > tile
        new_base = jnp.where(later, channels, 0)
        base = jnp.where(later, 0, channels)
        total_real = total_imag = None
        for start in range(0, channels, chunk):
            new_rows = pl.ds(pl.multiple_of(new_base + start, chunk), chunk)
            its_rows = pl.ds(pl.multiple_of(base + start, chunk), chunk)
            new_real, new_imag = fresh[new_index, new_rows, :rows], fresh[new_index, new_rows, rows:]
            real, imag = ref[index, its_rows, :rows], ref[index, its_rows, rows:]
            term_real = new_real * real + new_imag * imag
            term_imag = new_real * imag - new_imag * real
            total_real = term_real if total_real is None else total_real + term_real
            total_imag = term_imag if total_imag is None else total_imag + term_imag
        total_imag = total_imag * jnp.where(later, -1.0, 1.0)
        both = jnp.concatenate([total_real, total_imag], axis=1)
        if chunk > groups:
            both = sum(both[row : row + groups] for row in range(0, chunk, groups))
        offset = jnp.abs(new_tile - tile)
        sums[offset] = sums[offset] + both

    def each_new(new_index, carry):
        def each(ref, first):
            def body(index, carry):
                pair(ref, first, new_index, index)
                return carry

            return body

        lax.fori_loop(0, new_index + 1, each(fresh, 0), 0)
        first = len(new)
        for ref, old in zip(spectra, olds):
            lax.fori_loop(0, len(old), each(ref, first), 0)
            first += len(old)
        return carry

    lax.fori_loop(0, len(new), each_new, 0)
    if not last:
        out_ref[...] = sums[...]
        return
    real = jnp.concatenate([sums[offset, :, :rows] for offset in range(count)], axis=0)
    imag = jnp.concatenate([sums[offset, :, rows:] for offset in range(count)], axis=0)
    sign = 1.0 - 2.0 * (lax.broadcasted_iota(jnp.int32, real.shape, 1) % 2).astype(jnp.float32)
    none = jnp.zeros((groups, rows), jnp.float32)
    next_real = jnp.concatenate([real[groups:], none], axis=0) * sign
    next_imag = jnp.concatenate([imag[groups:], none], axis=0) * sign
    lags = jnp.dot(
        split(jnp.concatenate([real + next_imag, next_real - imag], axis=1)),
        inverse_ref[...],
        preferred_element_type=jnp.float32,
    )
    squares = jnp.broadcast_to(jnp.sum(lags * lags, keepdims=True), (8, rows))
    for offset in range(count):
        sums[offset, :, :rows] = lags[offset * groups : (offset + 1) * groups]
    for place in range(count):
        out_ref[place, :groups, :] = sums[lag_ref[place], :, :rows]
        out_ref[place, groups:, :] = squares


def absorb(blocks, new, spectra, olds, carried, me, tile_order, lag_order, count, last):
    rows, channels = blocks[0].shape[0], blocks[0].shape[1] // 2
    groups = channels // GROUP
    width = math.gcd(rows, 128)
    vmem = pl.BlockSpec(memory_space=pltpu.VMEM)
    smem = pl.BlockSpec(memory_space=pltpu.SMEM)
    tables = [jnp.asarray(forward_table(rows))] + ([jnp.asarray(inverse_table(rows))] if last else [])
    operands = tables + list(blocks) + list(spectra) + ([carried] if olds else [])
    out = (count, groups + 8, rows) if last else (count, groups, 2 * rows)
    fresh = jax.ShapeDtypeStruct((len(new), 2 * channels, 2 * rows), jnp.float32)
    result = pl.pallas_call(
        functools.partial(absorb_kernel, count, channels, rows, new, olds, last),
        out_shape=[jax.ShapeDtypeStruct(out, jnp.float32)] + ([] if last else [fresh]),
        in_specs=[smem, smem, smem] + [vmem] * len(operands),
        out_specs=[vmem] + ([] if last else [vmem]),
        scratch_shapes=([pltpu.VMEM(fresh.shape, jnp.float32)] if last else [])
        + [
            pltpu.VMEM((count, groups, 2 * rows), jnp.float32),
            pltpu.VMEM((rows // width, 2 * channels, width), jnp.float32),
            pltpu.SMEM((count,), jnp.int32),
        ],
        compiler_params=pltpu.CompilerParams(vmem_limit_bytes=20 * 2**20),
        cost_estimate=pl.CostEstimate(
            flops=24 * len(new) * rows * rows * channels, bytes_accessed=len(new) * rows * channels * 24, transcendentals=0
        ),
    )(me, tile_order, lag_order, *operands)
    return result[0] if last else result


def shards(inputs, out_grads, tile_order, lag_order):
    count = lax.axis_size("seq")
    rows = inputs.shape[0]
    channels = inputs.shape[1] // count
    groups = channels // GROUP
    me = lax.axis_index("seq").reshape(1)
    half = max(1, count // 2)
    far, near = list(range(count - 1, half - 1, -1)), list(range(half))
    blocks = dict(zip(far + near, cut(inputs, out_grads, me, count, far + near)))
    for step in far + near[1:]:
        pairs = [(place, partner(count, place, step)) for place in range(count)]
        blocks[step] = lax.ppermute(blocks[step], "seq", pairs)
    batch = max(1, len(far) // 4)
    later = far[:-batch]
    arrivals = [near[first : first + batch] + later[first : first + batch] for first in range(0, len(later), batch)]
    arrivals = [near[:batch] + far[:batch], near[batch:2*batch] + far[batch:2*batch], near[2*batch:] + far[2*batch:-batch], far[-batch:]]
    spectra, olds, carried = [], [], None
    for new in arrivals:
        last = new is arrivals[-1]
        made = absorb(
            [blocks[step] for step in new], new, spectra, list(olds), carried, me, tile_order, lag_order, count, last
        )
        if not last:
            carried, fresh = made
            spectra.append(fresh)
            olds.append(new)
    owned = lax.all_to_all(made, "seq", split_axis=0, concat_axis=0, tiled=True)
    squares = jnp.sum(owned[:, groups, :128], axis=0)
    ways = lax.axis_size("ch")
    total = squares
    for step in range(1, ways):
        total = total + lax.ppermute(squares, "ch", [(place, (place + step) % ways) for place in range(ways)])
    lags = owned[:, :groups, :].reshape(count * groups, rows)
    entries = ways * count * groups * count * rows
    factor = target_ratio * math.sqrt(entries) / jnp.sqrt(total[:1] + epsilon)
    return lags * factor


def solution(mesh):
    return jax.shard_map(
        shards,
        mesh=mesh,
        in_specs=(P("seq", "ch"), P("seq", "ch"), P(), P()),
        out_specs=P("ch", "seq"),
        check_vma=False,
    )
```

```python
import functools
import math

import jax
import jax.numpy as jnp
import ml_dtypes
import numpy as np
from jax import lax
from jax.experimental import pallas as pl
from jax.experimental.pallas import tpu as pltpu
from jax.sharding import PartitionSpec as P

GROUP = 16
target_ratio = 0.5
epsilon = 1e-12


def halves(table):
    high = table.astype(ml_dtypes.bfloat16)
    low = (table - high.astype(np.float64)).astype(ml_dtypes.bfloat16)
    return np.concatenate([high, high, low], axis=0)


def forward_table(rows):
    angles = np.outer(np.arange(rows), 2 * np.arange(rows) + 1) % (4 * rows) * (math.pi / (2 * rows))
    return halves(np.concatenate([np.cos(angles), -np.sin(angles)], axis=1))


def inverse_table(rows):
    angles = np.outer(2 * np.arange(rows) + 1, np.arange(rows)) % (4 * rows) * (math.pi / (2 * rows))
    return halves(np.concatenate([np.cos(angles), np.sin(angles)], axis=0) / rows)


def split(values):
    high = values.astype(jnp.bfloat16)
    low = (values - high.astype(jnp.float32)).astype(jnp.bfloat16)
    return jnp.concatenate([high, low, high], axis=1)


def partner(count, place, step, back=False):
    if count & (count - 1) == 0:
        return place ^ step
    return (place - step if back else place + step) % count


def cut_kernel(count, channels, steps, me_ref, inputs_ref, grads_ref, *refs):
    blocks, sems = refs[:-1], refs[-1]
    copies = []
    for index, step in enumerate(steps):
        start = pl.multiple_of(partner(count, me_ref[0], step) * channels, channels)
        for half, ref in enumerate((inputs_ref, grads_ref)):
            copies.append(
                pltpu.make_async_copy(
                    ref.at[:, pl.ds(start, channels)],
                    blocks[index].at[:, pl.ds(half * channels, channels)],
                    sems.at[2 * index + half],
                )
            )
    for copy in copies:
        copy.start()
    for copy in copies:
        copy.wait()


def cut(inputs, out_grads, me, count, steps):
    rows, channels = inputs.shape[0], inputs.shape[1] // count
    if channels % 128:
        blocks = []
        for step in steps:
            start = partner(count, me[0], step) * channels
            pair = [lax.dynamic_slice_in_dim(whole, start, channels, 1) for whole in (inputs, out_grads)]
            blocks.append(jnp.concatenate(pair, axis=1))
        return blocks
    anywhere = pl.BlockSpec(memory_space=pl.ANY)
    return pl.pallas_call(
        functools.partial(cut_kernel, count, channels, steps),
        out_shape=[pltpu.VMEM((rows, 2 * channels), jnp.float32) for _ in steps],
        in_specs=[pl.BlockSpec(memory_space=pltpu.SMEM), anywhere, anywhere],
        out_specs=[pl.BlockSpec(memory_space=pltpu.VMEM) for _ in steps],
        scratch_shapes=[pltpu.SemaphoreType.DMA((2 * len(steps),))],
        cost_estimate=pl.CostEstimate(flops=0, bytes_accessed=len(steps) * rows * channels * 16, transcendentals=0),
    )(me, inputs, out_grads)


def absorb_kernel(count, channels, rows, new, olds, last, me_ref, order_ref, lag_ref, forward_ref, *refs):
    refs = list(refs)
    take = lambda many: [refs.pop(0) for _ in range(many)]
    inverse_ref = take(1)[0] if last else None
    blocks, spectra = take(len(new)), take(len(olds))
    carried = take(1)[0] if olds else None
    out_ref = take(1)[0]
    fresh = take(1)[0]
    sums, turned, tile_of = take(3)
    width = turned.shape[2]
    groups = channels // GROUP
    chunk = max(8, groups)

    if carried is None:
        sums[...] = jnp.zeros_like(sums)
    else:
        sums[...] = carried[...]
    for index, step in enumerate(new):
        flipped = blocks[index][...].T
        columns = []
        for part in range(rows // width):
            turned[part] = flipped[:, part * width : (part + 1) * width]
            members = [
                turned[part, pl.ds(half * channels + member, groups, stride=GROUP), :]
                for half in range(2)
                for member in range(GROUP)
            ]
            columns.append(jnp.concatenate(members, axis=0))
        fresh[index] = jnp.dot(
            split(jnp.concatenate(columns, axis=1)), forward_ref[...], preferred_element_type=jnp.float32
        )
    slots = list(new) + [step for old in olds for step in old]
    for index, step in enumerate(slots):
        tile_of[index] = order_ref[partner(count, me_ref[0], step, back=True)]

    def pair(ref, first, new_index, index):
        new_tile, tile = tile_of[new_index], tile_of[first + index]
        later = new_tile > tile
        new_base = jnp.where(later, channels, 0)
        base = jnp.where(later, 0, channels)
        total_real = total_imag = None
        for start in range(0, channels, chunk):
            new_rows = pl.ds(pl.multiple_of(new_base + start, chunk), chunk)
            its_rows = pl.ds(pl.multiple_of(base + start, chunk), chunk)
            new_real, new_imag = fresh[new_index, new_rows, :rows], fresh[new_index, new_rows, rows:]
            real, imag = ref[index, its_rows, :rows], ref[index, its_rows, rows:]
            term_real = new_real * real + new_imag * imag
            term_imag = new_real * imag - new_imag * real
            total_real = term_real if total_real is None else total_real + term_real
            total_imag = term_imag if total_imag is None else total_imag + term_imag
        total_imag = total_imag * jnp.where(later, -1.0, 1.0)
        both = jnp.concatenate([total_real, total_imag], axis=1)
        if chunk > groups:
            both = sum(both[row : row + groups] for row in range(0, chunk, groups))
        offset = jnp.abs(new_tile - tile)
        sums[offset] = sums[offset] + both

    def each_new(new_index, carry):
        def each(ref, first):
            def body(index, carry):
                pair(ref, first, new_index, index)
                return carry

            return body

        lax.fori_loop(0, new_index + 1, each(fresh, 0), 0)
        first = len(new)
        for ref, old in zip(spectra, olds):
            lax.fori_loop(0, len(old), each(ref, first), 0)
            first += len(old)
        return carry

    lax.fori_loop(0, len(new), each_new, 0)
    if not last:
        out_ref[...] = sums[...]
        return
    real = jnp.concatenate([sums[offset, :, :rows] for offset in range(count)], axis=0)
    imag = jnp.concatenate([sums[offset, :, rows:] for offset in range(count)], axis=0)
    sign = 1.0 - 2.0 * (lax.broadcasted_iota(jnp.int32, real.shape, 1) % 2).astype(jnp.float32)
    none = jnp.zeros((groups, rows), jnp.float32)
    next_real = jnp.concatenate([real[groups:], none], axis=0) * sign
    next_imag = jnp.concatenate([imag[groups:], none], axis=0) * sign
    lags = jnp.dot(
        split(jnp.concatenate([real + next_imag, next_real - imag], axis=1)),
        inverse_ref[...],
        preferred_element_type=jnp.float32,
    )
    squares = jnp.broadcast_to(jnp.sum(lags * lags, keepdims=True), (8, rows))
    for offset in range(count):
        sums[offset, :, :rows] = lags[offset * groups : (offset + 1) * groups]
    for place in range(count):
        out_ref[place, :groups, :] = sums[lag_ref[place], :, :rows]
        out_ref[place, groups:, :] = squares


def absorb(blocks, new, spectra, olds, carried, me, tile_order, lag_order, count, last):
    rows, channels = blocks[0].shape[0], blocks[0].shape[1] // 2
    groups = channels // GROUP
    width = math.gcd(rows, 128)
    vmem = pl.BlockSpec(memory_space=pltpu.VMEM)
    smem = pl.BlockSpec(memory_space=pltpu.SMEM)
    tables = [jnp.asarray(forward_table(rows))] + ([jnp.asarray(inverse_table(rows))] if last else [])
    operands = tables + list(blocks) + list(spectra) + ([carried] if olds else [])
    out = (count, groups + 8, rows) if last else (count, groups, 2 * rows)
    fresh = jax.ShapeDtypeStruct((len(new), 2 * channels, 2 * rows), jnp.float32)
    result = pl.pallas_call(
        functools.partial(absorb_kernel, count, channels, rows, new, olds, last),
        out_shape=[jax.ShapeDtypeStruct(out, jnp.float32)] + ([] if last else [fresh]),
        in_specs=[smem, smem, smem] + [vmem] * len(operands),
        out_specs=[vmem] + ([] if last else [vmem]),
        scratch_shapes=([pltpu.VMEM(fresh.shape, jnp.float32)] if last else [])
        + [
            pltpu.VMEM((count, groups, 2 * rows), jnp.float32),
            pltpu.VMEM((rows // width, 2 * channels, width), jnp.float32),
            pltpu.SMEM((count,), jnp.int32),
        ],
        compiler_params=pltpu.CompilerParams(vmem_limit_bytes=20 * 2**20),
        cost_estimate=pl.CostEstimate(
            flops=24 * len(new) * rows * rows * channels, bytes_accessed=len(new) * rows * channels * 24, transcendentals=0
        ),
    )(me, tile_order, lag_order, *operands)
    return result[0] if last else result


def shards(inputs, out_grads, tile_order, lag_order):
    count = lax.axis_size("seq")
    rows = inputs.shape[0]
    channels = inputs.shape[1] // count
    groups = channels // GROUP
    me = lax.axis_index("seq").reshape(1)
    half = max(1, count // 2)
    far, near = list(range(count - 1, half - 1, -1)), list(range(half))
    first = cut(inputs, out_grads, me, count, far[:1])
    then, first = lax.optimization_barrier((me, first))
    blocks = dict(zip(far + near, first + cut(inputs, out_grads, then, count, far[1:] + near)))
    for step in far + near[1:]:
        pairs = [(place, partner(count, place, step)) for place in range(count)]
        blocks[step] = lax.ppermute(blocks[step], "seq", pairs)
    batch = max(1, count // 8)
    arrivals = [near[:batch] + far[:batch]]
    arrivals.append(near[batch : 2 * batch] + far[batch : 2 * batch])
    arrivals.append(near[2 * batch :])
    arrivals.append(far[2 * batch : -batch])
    arrivals.append(far[-batch:])
    spectra, olds, carried = [], [], None
    for new in arrivals:
        last = new is arrivals[-1]
        made = absorb(
            [blocks[step] for step in new], new, spectra, list(olds), carried, me, tile_order, lag_order, count, last
        )
        if not last:
            carried, fresh = made
            spectra.append(fresh)
            olds.append(new)
    owned = lax.all_to_all(made, "seq", split_axis=0, concat_axis=0, tiled=True)
    squares = jnp.sum(owned[:, groups, :128], axis=0)
    ways = lax.axis_size("ch")
    total = squares
    for step in range(1, ways):
        total = total + lax.ppermute(squares, "ch", [(place, (place + step) % ways) for place in range(ways)])
    lags = owned[:, :groups, :].reshape(count * groups, rows)
    entries = ways * count * groups * count * rows
    factor = target_ratio * math.sqrt(entries) / jnp.sqrt(total[:1] + epsilon)
    return lags * factor


def solution(mesh):
    return jax.shard_map(
        shards,
        mesh=mesh,
        in_specs=(P("seq", "ch"), P("seq", "ch"), P(), P()),
        out_specs=P("ch", "seq"),
        check_vma=False,
    )
```

```python
import functools
import math

import jax
import jax.numpy as jnp
import ml_dtypes
import numpy as np
from jax import lax
from jax.experimental import pallas as pl
from jax.experimental.pallas import tpu as pltpu
from jax.sharding import PartitionSpec as P

GROUP = 16
target_ratio = 0.5
epsilon = 1e-12


def halves(table):
    high = table.astype(ml_dtypes.bfloat16)
    low = (table - high.astype(np.float64)).astype(ml_dtypes.bfloat16)
    return np.concatenate([high, high, low], axis=0)


def forward_table(rows):
    angles = np.outer(np.arange(rows), 2 * np.arange(rows) + 1) % (4 * rows) * (math.pi / (2 * rows))
    return halves(np.concatenate([np.cos(angles), -np.sin(angles)], axis=1))


def inverse_table(rows):
    angles = np.outer(2 * np.arange(rows) + 1, np.arange(rows)) % (4 * rows) * (math.pi / (2 * rows))
    return halves(np.concatenate([np.cos(angles), np.sin(angles)], axis=0) / rows)


def split(values):
    high = values.astype(jnp.bfloat16)
    low = (values - high.astype(jnp.float32)).astype(jnp.bfloat16)
    return jnp.concatenate([high, low, high], axis=1)


def partner(count, place, step, back=False):
    if count & (count - 1) == 0:
        return place ^ step
    return (place - step if back else place + step) % count


def cut_kernel(count, channels, steps, inputs_ref, grads_ref, *refs):
    me = lax.axis_index("seq")
    blocks, sems = refs[:-1], refs[-1]
    copies = []
    for index, step in enumerate(steps):
        start = pl.multiple_of(partner(count, me, step) * channels, channels)
        for half, ref in enumerate((inputs_ref, grads_ref)):
            copies.append(
                pltpu.make_async_copy(
                    ref.at[:, pl.ds(start, channels)],
                    blocks[index].at[:, pl.ds(half * channels, channels)],
                    sems.at[2 * index + half],
                )
            )
    for copy in copies:
        copy.start()
    for copy in copies:
        copy.wait()


def cut(inputs, out_grads, count, steps):
    rows, channels = inputs.shape[0], inputs.shape[1] // count
    if channels % 128:
        blocks = []
        for step in steps:
            start = partner(count, lax.axis_index("seq"), step) * channels
            pair = [lax.dynamic_slice_in_dim(whole, start, channels, 1) for whole in (inputs, out_grads)]
            blocks.append(jnp.concatenate(pair, axis=1))
        return blocks
    anywhere = pl.BlockSpec(memory_space=pl.ANY)
    return pl.pallas_call(
        functools.partial(cut_kernel, count, channels, steps),
        out_shape=[jax.ShapeDtypeStruct((rows, 2 * channels), jnp.float32) for _ in steps],
        in_specs=[anywhere, anywhere],
        out_specs=[pl.BlockSpec(memory_space=pltpu.VMEM) for _ in steps],
        scratch_shapes=[pltpu.SemaphoreType.DMA((2 * len(steps),))],
        compiler_params=pltpu.CompilerParams(vmem_limit_bytes=6 * 2**20),
        cost_estimate=pl.CostEstimate(flops=0, bytes_accessed=len(steps) * rows * channels * 16, transcendentals=0),
    )(*(pltpu.with_memory_space_constraint(whole, pltpu.HBM) for whole in (inputs, out_grads)))


def absorb_kernel(count, channels, rows, new, olds, inner, last, order_ref, lag_ref, forward_ref, *refs):
    refs = list(refs)
    take = lambda many: [refs.pop(0) for _ in range(many)]
    inverse_ref = take(1)[0] if last else None
    blocks, spectra = take(len(new)), take(len(olds))
    carried = take(1)[0] if olds else None
    out_ref = take(1)[0]
    fresh = take(1)[0]
    sums, turned, tile_of = take(3)
    width = turned.shape[2]
    groups = channels // GROUP
    chunk = max(8, groups)

    if carried is None:
        sums[...] = jnp.zeros_like(sums)
    else:
        sums[...] = carried[...]
    for index, step in enumerate(new):
        flipped = blocks[index][...].T
        columns = []
        for part in range(rows // width):
            turned[part] = flipped[:, part * width : (part + 1) * width]
            members = [
                turned[part, pl.ds(half * channels + member, groups, stride=GROUP), :]
                for half in range(2)
                for member in range(GROUP)
            ]
            columns.append(jnp.concatenate(members, axis=0))
        fresh[index] = jnp.dot(
            split(jnp.concatenate(columns, axis=1)), forward_ref[...], preferred_element_type=jnp.float32
        )
    slots = list(new) + [step for old in olds for step in old]
    for index, step in enumerate(slots):
        tile_of[index] = order_ref[partner(count, lax.axis_index("seq"), step, back=True)]

    def pair(ref, first, new_index, index):
        new_tile, tile = tile_of[new_index], tile_of[first + index]
        later = new_tile > tile
        new_base = jnp.where(later, channels, 0)
        base = jnp.where(later, 0, channels)
        total_real = total_imag = None
        for start in range(0, channels, chunk):
            new_rows = pl.ds(pl.multiple_of(new_base + start, chunk), chunk)
            its_rows = pl.ds(pl.multiple_of(base + start, chunk), chunk)
            new_real, new_imag = fresh[new_index, new_rows, :rows], fresh[new_index, new_rows, rows:]
            real, imag = ref[index, its_rows, :rows], ref[index, its_rows, rows:]
            term_real = new_real * real + new_imag * imag
            term_imag = new_real * imag - new_imag * real
            total_real = term_real if total_real is None else total_real + term_real
            total_imag = term_imag if total_imag is None else total_imag + term_imag
        total_imag = total_imag * jnp.where(later, -1.0, 1.0)
        both = jnp.concatenate([total_real, total_imag], axis=1)
        if chunk > groups:
            both = sum(both[row : row + groups] for row in range(0, chunk, groups))
        offset = jnp.abs(new_tile - tile)
        sums[offset] = sums[offset] + both

    def each_new(new_index, carry):
        def each(ref, first):
            def body(index, carry):
                pair(ref, first, new_index, index)
                return carry

            return body

        lax.fori_loop(0, new_index + 1, each(fresh, 0), 0)
        first = len(new)
        for ref, old in zip(spectra, olds):
            lax.fori_loop(0, len(old), each(ref, first), 0)
            first += len(old)
        return carry

    lax.fori_loop(0, len(new), each_new, 0)
    if not last:
        out_ref[...] = sums[...]
        return
    real = jnp.concatenate([sums[offset, :, :rows] for offset in range(count)], axis=0)
    imag = jnp.concatenate([sums[offset, :, rows:] for offset in range(count)], axis=0)
    sign = 1.0 - 2.0 * (lax.broadcasted_iota(jnp.int32, real.shape, 1) % 2).astype(jnp.float32)
    none = jnp.zeros((groups, rows), jnp.float32)
    next_real = jnp.concatenate([real[groups:], none], axis=0) * sign
    next_imag = jnp.concatenate([imag[groups:], none], axis=0) * sign
    lags = jnp.dot(
        split(jnp.concatenate([real + next_imag, next_real - imag], axis=1)),
        inverse_ref[...],
        preferred_element_type=jnp.float32,
    )
    squares = jnp.broadcast_to(jnp.sum(lags * lags, keepdims=True), (1, out_ref.shape[2] - groups * rows))
    for offset in range(count):
        sums[offset, :, :rows] = lags[offset * groups : (offset + 1) * groups]
    ways = out_ref.shape[0] // count
    way = lax.axis_index("ch") // inner
    for piece in range(count * ways):
        out_ref[piece, :, groups * rows :] = squares
        out_ref[piece, :, : groups * rows] = jnp.zeros((1, groups * rows), jnp.float32)
    for place in range(count):
        block = sums[lag_ref[place], :, :rows]
        for group in range(groups):
            out_ref[place * ways + way, :, group * rows : (group + 1) * rows] = block[group : group + 1]


def gather_kernel(count, groups, rows, inner, owned_ref, out_ref):
    ways = owned_ref.shape[0] // count
    way = lax.axis_index("ch") // inner
    for place in range(count):
        for group in range(groups):
            row = owned_ref[place * ways + way, :, group * rows : (group + 1) * rows]
            out_ref[place * groups + group : place * groups + group + 1, :] = row


def gather(owned, count, groups, rows, inner):
    vmem = pl.BlockSpec(memory_space=pltpu.VMEM)
    return pl.pallas_call(
        functools.partial(gather_kernel, count, groups, rows, inner),
        out_shape=jax.ShapeDtypeStruct((count * groups, rows), jnp.float32),
        in_specs=[vmem],
        out_specs=vmem,
        compiler_params=pltpu.CompilerParams(vmem_limit_bytes=4 * 2**20),
        cost_estimate=pl.CostEstimate(flops=0, bytes_accessed=count * groups * rows * 8, transcendentals=0),
    )(owned)


def absorb(blocks, new, spectra, olds, carried, tile_order, lag_order, count, ways, inner, last):
    rows, channels = blocks[0].shape[0], blocks[0].shape[1] // 2
    groups = channels // GROUP
    width = math.gcd(rows, 128)
    vmem = pl.BlockSpec(memory_space=pltpu.VMEM)
    smem = pl.BlockSpec(memory_space=pltpu.SMEM)
    tables = [jnp.asarray(forward_table(rows))] + ([jnp.asarray(inverse_table(rows))] if last else [])
    operands = tables + list(blocks) + list(spectra) + ([carried] if olds else [])
    out = (count * ways, 1, groups * rows + 128) if last else (count, groups, 2 * rows)
    fresh = jax.ShapeDtypeStruct((len(new), 2 * channels, 2 * rows), jnp.float32)
    result = pl.pallas_call(
        functools.partial(absorb_kernel, count, channels, rows, new, olds, inner, last),
        out_shape=[jax.ShapeDtypeStruct(out, jnp.float32)] + ([] if last else [fresh]),
        in_specs=[smem, smem] + [vmem] * len(operands),
        out_specs=[vmem] + ([] if last else [vmem]),
        scratch_shapes=([pltpu.VMEM(fresh.shape, jnp.float32)] if last else [])
        + [
            pltpu.VMEM((count, groups, 2 * rows), jnp.float32),
            pltpu.VMEM((rows // width, 2 * channels, width), jnp.float32),
            pltpu.SMEM((count,), jnp.int32),
        ],
        compiler_params=pltpu.CompilerParams(vmem_limit_bytes=20 * 2**20),
        cost_estimate=pl.CostEstimate(
            flops=24 * len(new) * rows * rows * channels, bytes_accessed=len(new) * rows * channels * 24, transcendentals=0
        ),
    )(tile_order, lag_order, *operands)
    return result[0] if last else result


def shards(inputs, out_grads, tile_order, lag_order):
    count = lax.axis_size("seq")
    rows = inputs.shape[0]
    channels = inputs.shape[1] // count
    groups = channels // GROUP
    ways = lax.axis_size("ch")
    inner = 2 if ways % 2 == 0 else 1
    outer = ways // inner
    half = max(1, count // 2)
    far, near = list(range(count - 1, half - 1, -1)), list(range(half))
    first = cut(inputs, out_grads, count, far[:1])
    inputs, out_grads, first = lax.optimization_barrier((inputs, out_grads, first))
    blocks = dict(zip(far + near, first + cut(inputs, out_grads, count, far[1:] + near)))
    for step in far + near[1:]:
        pairs = [(place, partner(count, place, step)) for place in range(count)]
        blocks[step] = lax.ppermute(blocks[step], "seq", pairs)
    batch = max(1, count // 8)
    arrivals = [near[:batch] + far[:batch]]
    arrivals.append(near[batch : 2 * batch] + far[batch : 2 * batch])
    arrivals.append(near[2 * batch :])
    arrivals.append(far[2 * batch : -batch])
    arrivals.append(far[-batch:])
    spectra, olds, carried = [], [], None
    for new in arrivals:
        last = new is arrivals[-1]
        made = absorb(
            [blocks[step] for step in new],
            new,
            spectra,
            list(olds),
            carried,
            tile_order,
            lag_order,
            count,
            outer,
            inner,
            last,
        )
        if not last:
            carried, fresh = made
            spectra.append(fresh)
            olds.append(new)
    together = [
        [place * ways + way * inner + core for place in range(count) for way in range(outer)] for core in range(inner)
    ]
    owned = lax.all_to_all(
        made, ("seq", "ch"), split_axis=0, concat_axis=0, axis_index_groups=together, tiled=True
    )
    squares = owned[:, :, groups * rows :]
    if inner == 2:
        pairs = [(place, place ^ 1) for place in range(ways)]
        squares = squares + lax.ppermute(squares, "ch", pairs)
    total = jnp.sum(squares, axis=(0, 1))
    lags = gather(owned, count, groups, rows, inner)
    entries = ways * count * groups * count * rows
    factor = target_ratio * math.sqrt(entries) / jnp.sqrt(total[:1] + epsilon)
    return lags * factor


def solution(mesh):
    return jax.shard_map(
        shards,
        mesh=mesh,
        in_specs=(P("seq", "ch"), P("seq", "ch"), P(), P()),
        out_specs=P("ch", "seq"),
        check_vma=False,
    )
```

```python
import functools
import math

import jax
import jax.numpy as jnp
import ml_dtypes
import numpy as np
from jax import lax
from jax.experimental import pallas as pl
from jax.experimental.pallas import tpu as pltpu
from jax.sharding import PartitionSpec as P

GROUP = 16
target_ratio = 0.5
epsilon = 1e-12


def halves(table):
    high = table.astype(ml_dtypes.bfloat16)
    low = (table - high.astype(np.float64)).astype(ml_dtypes.bfloat16)
    return np.concatenate([high, high, low], axis=0)


def forward_table(rows):
    angles = np.outer(np.arange(rows), 2 * np.arange(rows) + 1) % (4 * rows) * (math.pi / (2 * rows))
    return halves(np.concatenate([np.cos(angles), -np.sin(angles)], axis=1))


def inverse_table(rows):
    angles = np.outer(2 * np.arange(rows) + 1, np.arange(rows)) % (4 * rows) * (math.pi / (2 * rows))
    return halves(np.concatenate([np.cos(angles), np.sin(angles)], axis=0) / rows)


def split(values):
    high = values.astype(jnp.bfloat16)
    low = (values - high.astype(jnp.float32)).astype(jnp.bfloat16)
    return jnp.concatenate([high, low, high], axis=1)


def partner(count, place, step, back=False):
    if count & (count - 1) == 0:
        return place ^ step
    return (place - step if back else place + step) % count


def cut_kernel(count, channels, steps, inputs_ref, grads_ref, *refs):
    me = lax.axis_index("seq")
    blocks, sems = refs[:-1], refs[-1]
    copies = []
    for index, step in enumerate(steps):
        start = pl.multiple_of(partner(count, me, step) * channels, channels)
        for half, ref in enumerate((inputs_ref, grads_ref)):
            copies.append(
                pltpu.make_async_copy(
                    ref.at[:, pl.ds(start, channels)],
                    blocks[index].at[:, pl.ds(half * channels, channels)],
                    sems.at[2 * index + half],
                )
            )
    for copy in copies:
        copy.start()
    for copy in copies:
        copy.wait()


def cut(inputs, out_grads, count, steps):
    rows, channels = inputs.shape[0], inputs.shape[1] // count
    if channels % 128:
        blocks = []
        for step in steps:
            start = partner(count, lax.axis_index("seq"), step) * channels
            pair = [lax.dynamic_slice_in_dim(whole, start, channels, 1) for whole in (inputs, out_grads)]
            blocks.append(jnp.concatenate(pair, axis=1))
        return blocks
    anywhere = pl.BlockSpec(memory_space=pl.ANY)
    return pl.pallas_call(
        functools.partial(cut_kernel, count, channels, steps),
        out_shape=[jax.ShapeDtypeStruct((rows, 2 * channels), jnp.float32) for _ in steps],
        in_specs=[anywhere, anywhere],
        out_specs=[pl.BlockSpec(memory_space=pltpu.VMEM) for _ in steps],
        scratch_shapes=[pltpu.SemaphoreType.DMA((2 * len(steps),))],
        compiler_params=pltpu.CompilerParams(vmem_limit_bytes=6 * 2**20),
        cost_estimate=pl.CostEstimate(flops=0, bytes_accessed=len(steps) * rows * channels * 16, transcendentals=0),
    )(*(pltpu.with_memory_space_constraint(whole, pltpu.HBM) for whole in (inputs, out_grads)))


def absorb_kernel(count, channels, rows, new, olds, inner, last, order_from, lag_from, forward_ref, *refs):
    refs = list(refs)
    take = lambda many: [refs.pop(0) for _ in range(many)]
    inverse_ref = take(1)[0] if last else None
    blocks, spectra = take(len(new)), take(len(olds))
    carried = take(1)[0] if olds else None
    out_ref = take(1)[0]
    fresh = take(1)[0]
    sums, turned, order_ref, lag_ref, tile_of, sems = take(6)
    width = turned.shape[2]
    scalars = [pltpu.make_async_copy(order_from, order_ref, sems.at[0])]
    if last:
        scalars.append(pltpu.make_async_copy(lag_from, lag_ref, sems.at[1]))
    for copy in scalars:
        copy.start()
    groups = channels // GROUP
    chunk = max(8, groups)

    if carried is None:
        sums[...] = jnp.zeros_like(sums)
    else:
        sums[...] = carried[...]
    for index, step in enumerate(new):
        flipped = blocks[index][...].T
        columns = []
        for part in range(rows // width):
            turned[part] = flipped[:, part * width : (part + 1) * width]
            members = [
                turned[part, pl.ds(half * channels + member, groups, stride=GROUP), :]
                for half in range(2)
                for member in range(GROUP)
            ]
            columns.append(jnp.concatenate(members, axis=0))
        fresh[index] = jnp.dot(
            split(jnp.concatenate(columns, axis=1)), forward_ref[...], preferred_element_type=jnp.float32
        )
    for copy in scalars:
        copy.wait()
    slots = list(new) + [step for old in olds for step in old]
    for index, step in enumerate(slots):
        tile_of[index] = order_ref[partner(count, lax.axis_index("seq"), step, back=True)]

    def meet(new_index, others):
        new_tile = tile_of[new_index]
        tiles = [tile_of[place] for place, _, _ in others]
        later = [jnp.full((chunk, rows), (new_tile > tile).astype(jnp.int32)) > 0 for tile in tiles]
        bases = [jnp.where(new_tile > tile, 0, channels) for tile in tiles]

        def step(index, totals):
            start = index * chunk
            input_rows = slice(start, start + chunk)
            grad_rows = slice(channels + start, channels + start + chunk)
            input_real, input_imag = fresh[new_index, input_rows, :rows], fresh[new_index, input_rows, rows:]
            grad_real, grad_imag = fresh[new_index, grad_rows, :rows], fresh[new_index, grad_rows, rows:]
            out = []
            for (_, ref, slot), is_later, base, (total_real, total_imag) in zip(others, later, bases, totals):
                its_rows = pl.ds(pl.multiple_of(base + start, chunk), chunk)
                real, imag = ref[slot, its_rows, :rows], ref[slot, its_rows, rows:]
                new_real = jnp.where(is_later, grad_real, input_real)
                new_imag = jnp.where(is_later, grad_imag, input_imag)
                out.append(
                    (
                        total_real + (new_real * real + new_imag * imag),
                        total_imag + (new_real * imag - new_imag * real),
                    )
                )
            return out

        zero = jnp.zeros((chunk, rows), jnp.float32)
        totals = [(zero, zero) for _ in others]
        for index in range(channels // chunk):
            totals = step(index, totals)
        for tile, (total_real, total_imag) in zip(tiles, totals):
            total_imag = total_imag * jnp.where(new_tile > tile, -1.0, 1.0)
            both = jnp.concatenate([total_real, total_imag], axis=1)
            if chunk > groups:
                both = sum(both[row : row + groups] for row in range(0, chunk, groups))
            offset = jnp.abs(new_tile - tile)
            sums[offset] = sums[offset] + both

    earlier = [(ref, slot) for ref, old in zip(spectra, olds) for slot in range(len(old))]
    for new_index in range(len(new)):
        others = [(place, fresh, place) for place in range(new_index + 1)]
        others += [(len(new) + place, ref, slot) for place, (ref, slot) in enumerate(earlier)]
        for first in range(0, len(others), 4):
            meet(new_index, others[first : first + 4])
    if not last:
        out_ref[...] = sums[...]
        return
    real = jnp.concatenate([sums[offset, :, :rows] for offset in range(count)], axis=0)
    imag = jnp.concatenate([sums[offset, :, rows:] for offset in range(count)], axis=0)
    sign = 1.0 - 2.0 * (lax.broadcasted_iota(jnp.int32, real.shape, 1) % 2).astype(jnp.float32)
    none = jnp.zeros((groups, rows), jnp.float32)
    next_real = jnp.concatenate([real[groups:], none], axis=0) * sign
    next_imag = jnp.concatenate([imag[groups:], none], axis=0) * sign
    lags = jnp.dot(
        split(jnp.concatenate([real + next_imag, next_real - imag], axis=1)),
        inverse_ref[...],
        preferred_element_type=jnp.float32,
    )
    squares = jnp.broadcast_to(jnp.sum(lags * lags, keepdims=True), (1, out_ref.shape[2] - groups * rows))
    for offset in range(count):
        sums[offset, :, :rows] = lags[offset * groups : (offset + 1) * groups]
    ways = out_ref.shape[0] // count
    way = lax.axis_index("ch") // inner
    for piece in range(count * ways):
        out_ref[piece, :, groups * rows :] = squares
        out_ref[piece, :, : groups * rows] = jnp.zeros((1, groups * rows), jnp.float32)
    for place in range(count):
        block = sums[lag_ref[place], :, :rows]
        for group in range(groups):
            out_ref[place * ways + way, :, group * rows : (group + 1) * rows] = block[group : group + 1]


def gather_kernel(count, groups, rows, inner, owned_ref, out_ref):
    ways = owned_ref.shape[0] // count
    way = lax.axis_index("ch") // inner
    for place in range(count):
        for group in range(groups):
            row = owned_ref[place * ways + way, :, group * rows : (group + 1) * rows]
            out_ref[place * groups + group : place * groups + group + 1, :] = row


def gather(owned, count, groups, rows, inner):
    vmem = pl.BlockSpec(memory_space=pltpu.VMEM)
    return pl.pallas_call(
        functools.partial(gather_kernel, count, groups, rows, inner),
        out_shape=jax.ShapeDtypeStruct((count * groups, rows), jnp.float32),
        in_specs=[vmem],
        out_specs=vmem,
        compiler_params=pltpu.CompilerParams(vmem_limit_bytes=4 * 2**20),
        cost_estimate=pl.CostEstimate(flops=0, bytes_accessed=count * groups * rows * 8, transcendentals=0),
    )(owned)


def absorb(blocks, new, spectra, olds, carried, tile_order, lag_order, count, ways, inner, last):
    rows, channels = blocks[0].shape[0], blocks[0].shape[1] // 2
    groups = channels // GROUP
    width = math.gcd(rows, 128)
    vmem = pl.BlockSpec(memory_space=pltpu.VMEM)
    anywhere = pl.BlockSpec(memory_space=pl.ANY)
    tables = [jnp.asarray(forward_table(rows))] + ([jnp.asarray(inverse_table(rows))] if last else [])
    operands = tables + list(blocks) + list(spectra) + ([carried] if olds else [])
    out = (count * ways, 1, groups * rows + 128) if last else (count, groups, 2 * rows)
    fresh = jax.ShapeDtypeStruct((len(new), 2 * channels, 2 * rows), jnp.float32)
    result = pl.pallas_call(
        functools.partial(absorb_kernel, count, channels, rows, new, olds, inner, last),
        out_shape=[jax.ShapeDtypeStruct(out, jnp.float32)] + ([] if last else [fresh]),
        in_specs=[anywhere, anywhere] + [vmem] * len(operands),
        out_specs=[vmem] + ([] if last else [vmem]),
        scratch_shapes=([pltpu.VMEM(fresh.shape, jnp.float32)] if last else [])
        + [
            pltpu.VMEM((count, groups, 2 * rows), jnp.float32),
            pltpu.VMEM((rows // width, 2 * channels, width), jnp.float32),
            pltpu.SMEM((count,), jnp.int32),
            pltpu.SMEM((count,), jnp.int32),
            pltpu.SMEM((count,), jnp.int32),
            pltpu.SemaphoreType.DMA((2,)),
        ],
        compiler_params=pltpu.CompilerParams(vmem_limit_bytes=20 * 2**20),
        cost_estimate=pl.CostEstimate(
            flops=24 * len(new) * rows * rows * channels, bytes_accessed=len(new) * rows * channels * 24, transcendentals=0
        ),
    )(tile_order, lag_order, *operands)
    return result[0] if last else result


def shards(inputs, out_grads, tile_order, lag_order):
    count = lax.axis_size("seq")
    rows = inputs.shape[0]
    channels = inputs.shape[1] // count
    groups = channels // GROUP
    ways = lax.axis_size("ch")
    inner = 2 if ways % 2 == 0 else 1
    outer = ways // inner
    half = max(1, count // 2)
    far, near = list(range(count - 1, half - 1, -1)), list(range(half))
    first = cut(inputs, out_grads, count, far[:1])
    inputs, out_grads, first = lax.optimization_barrier((inputs, out_grads, first))
    blocks = dict(zip(far + near, first + cut(inputs, out_grads, count, far[1:] + near)))
    for step in far + near[1:]:
        pairs = [(place, partner(count, place, step)) for place in range(count)]
        blocks[step] = lax.ppermute(blocks[step], "seq", pairs)
    batch = max(1, count // 8)
    arrivals = [near[:batch] + far[:batch]]
    arrivals.append(near[batch : 2 * batch] + far[batch : 2 * batch])
    arrivals.append(near[2 * batch :])
    arrivals.append(far[2 * batch : -batch])
    arrivals.append(far[-batch:])
    spectra, olds, carried = [], [], None
    for new in arrivals:
        last = new is arrivals[-1]
        made = absorb(
            [blocks[step] for step in new],
            new,
            spectra,
            list(olds),
            carried,
            tile_order,
            lag_order,
            count,
            outer,
            inner,
            last,
        )
        if not last:
            carried, fresh = made
            spectra.append(fresh)
            olds.append(new)
    together = [
        [place * ways + way * inner + core for place in range(count) for way in range(outer)] for core in range(inner)
    ]
    owned = lax.all_to_all(
        made, ("seq", "ch"), split_axis=0, concat_axis=0, axis_index_groups=together, tiled=True
    )
    squares = owned[:, :, groups * rows :]
    if inner == 2:
        pairs = [(place, place ^ 1) for place in range(ways)]
        squares = squares + lax.ppermute(squares, "ch", pairs)
    total = jnp.sum(squares, axis=(0, 1))
    lags = gather(owned, count, groups, rows, inner)
    entries = ways * count * groups * count * rows
    factor = target_ratio * math.sqrt(entries) / jnp.sqrt(total[:1] + epsilon)
    return lags * factor


def solution(mesh):
    return jax.shard_map(
        shards,
        mesh=mesh,
        in_specs=(P("seq", "ch"), P("seq", "ch"), P(), P()),
        out_specs=P("ch", "seq"),
        check_vma=False,
    )
```

```python
import functools
import math

import jax
import jax.numpy as jnp
import ml_dtypes
import numpy as np
from jax import lax
from jax.experimental import pallas as pl
from jax.experimental.pallas import tpu as pltpu
from jax.sharding import PartitionSpec as P

GROUP = 16
target_ratio = 0.5
epsilon = 1e-12


def halves(table):
    high = table.astype(ml_dtypes.bfloat16)
    low = (table - high.astype(np.float64)).astype(ml_dtypes.bfloat16)
    return np.concatenate([high, high, low], axis=0)


def forward_table(rows):
    angles = np.outer(np.arange(rows), 2 * np.arange(rows) + 1) % (4 * rows) * (math.pi / (2 * rows))
    return halves(np.concatenate([np.cos(angles), -np.sin(angles)], axis=1))


def inverse_table(rows):
    angles = np.outer(2 * np.arange(rows) + 1, np.arange(rows)) % (4 * rows) * (math.pi / (2 * rows))
    return halves(np.concatenate([np.cos(angles), np.sin(angles)], axis=0) / rows)


def split(values):
    high = values.astype(jnp.bfloat16)
    low = (values - high.astype(jnp.float32)).astype(jnp.bfloat16)
    return jnp.concatenate([high, low, high], axis=1)


def partner(count, place, step, back=False):
    if count & (count - 1) == 0:
        return place ^ step
    return (place - step if back else place + step) % count


def cut_kernel(count, channels, steps, inputs_ref, grads_ref, *refs):
    me = lax.axis_index("seq")
    blocks, sems = refs[:-1], refs[-1]
    copies = []
    for index, step in enumerate(steps):
        start = pl.multiple_of(partner(count, me, step) * channels, channels)
        for half, ref in enumerate((inputs_ref, grads_ref)):
            copies.append(
                pltpu.make_async_copy(
                    ref.at[:, pl.ds(start, channels)],
                    blocks[index].at[:, pl.ds(half * channels, channels)],
                    sems.at[2 * index + half],
                )
            )
    for copy in copies:
        copy.start()
    for copy in copies:
        copy.wait()


def cut(inputs, out_grads, count, steps):
    rows, channels = inputs.shape[0], inputs.shape[1] // count
    if channels % 128:
        blocks = []
        for step in steps:
            start = partner(count, lax.axis_index("seq"), step) * channels
            pair = [lax.dynamic_slice_in_dim(whole, start, channels, 1) for whole in (inputs, out_grads)]
            blocks.append(jnp.concatenate(pair, axis=1))
        return blocks
    anywhere = pl.BlockSpec(memory_space=pl.ANY)
    return pl.pallas_call(
        functools.partial(cut_kernel, count, channels, steps),
        out_shape=[jax.ShapeDtypeStruct((rows, 2 * channels), jnp.float32) for _ in steps],
        in_specs=[anywhere, anywhere],
        out_specs=[pl.BlockSpec(memory_space=pltpu.VMEM) for _ in steps],
        scratch_shapes=[pltpu.SemaphoreType.DMA((2 * len(steps),))],
        compiler_params=pltpu.CompilerParams(vmem_limit_bytes=6 * 2**20),
        cost_estimate=pl.CostEstimate(flops=0, bytes_accessed=len(steps) * rows * channels * 16, transcendentals=0),
    )(*(pltpu.with_memory_space_constraint(whole, pltpu.HBM) for whole in (inputs, out_grads)))


def absorb_kernel(count, channels, rows, new, olds, inner, last, order_from, lag_from, forward_ref, *refs):
    refs = list(refs)
    take = lambda many: [refs.pop(0) for _ in range(many)]
    inverse_ref = take(1)[0] if last else None
    blocks, spectra = take(len(new)), take(len(olds))
    carried = take(1)[0] if olds else None
    out_ref = take(1)[0]
    fresh = take(1)[0]
    sums, turned, order_ref, lag_ref, tile_of, sems = take(6)
    width = turned.shape[2]
    scalars = [pltpu.make_async_copy(order_from, order_ref, sems.at[0])]
    if last:
        scalars.append(pltpu.make_async_copy(lag_from, lag_ref, sems.at[1]))
    for copy in scalars:
        copy.start()
    groups = channels // GROUP
    chunk = max(8, groups)

    if carried is None:
        sums[...] = jnp.zeros_like(sums)
    else:
        sums[...] = carried[...]
    for index, step in enumerate(new):
        flipped = blocks[index][...].T
        columns = []
        for part in range(rows // width):
            turned[part] = flipped[:, part * width : (part + 1) * width]
            members = [
                turned[part, pl.ds(half * channels + member, groups, stride=GROUP), :]
                for half in range(2)
                for member in range(GROUP)
            ]
            columns.append(jnp.concatenate(members, axis=0))
        fresh[index] = jnp.dot(
            split(jnp.concatenate(columns, axis=1)), forward_ref[...], preferred_element_type=jnp.float32
        )
    for copy in scalars:
        copy.wait()
    slots = list(new) + [step for old in olds for step in old]
    for index, step in enumerate(slots):
        tile_of[index] = order_ref[partner(count, lax.axis_index("seq"), step, back=True)]

    def meet(new_index, others):
        new_tile = tile_of[new_index]
        tiles = [tile_of[place] for place, _, _ in others]
        later = [jnp.full((chunk, rows), (new_tile > tile).astype(jnp.int32)) > 0 for tile in tiles]
        bases = [jnp.where(new_tile > tile, 0, channels) for tile in tiles]

        def step(index, totals):
            start = index * chunk
            input_rows = slice(start, start + chunk)
            grad_rows = slice(channels + start, channels + start + chunk)
            input_real, input_imag = fresh[new_index, input_rows, :rows], fresh[new_index, input_rows, rows:]
            grad_real, grad_imag = fresh[new_index, grad_rows, :rows], fresh[new_index, grad_rows, rows:]
            out = []
            for (_, ref, slot), is_later, base, (total_real, total_imag) in zip(others, later, bases, totals):
                its_rows = pl.ds(pl.multiple_of(base + start, chunk), chunk)
                real, imag = ref[slot, its_rows, :rows], ref[slot, its_rows, rows:]
                new_real = jnp.where(is_later, grad_real, input_real)
                new_imag = jnp.where(is_later, grad_imag, input_imag)
                out.append(
                    (
                        total_real + (new_real * real + new_imag * imag),
                        total_imag + (new_real * imag - new_imag * real),
                    )
                )
            return out

        zero = jnp.zeros((chunk, rows), jnp.float32)
        totals = [(zero, zero) for _ in others]
        for index in range(channels // chunk):
            totals = step(index, totals)
        for tile, (total_real, total_imag) in zip(tiles, totals):
            total_imag = total_imag * jnp.where(new_tile > tile, -1.0, 1.0)
            both = jnp.concatenate([total_real, total_imag], axis=1)
            if chunk > groups:
                both = sum(both[row : row + groups] for row in range(0, chunk, groups))
            offset = jnp.abs(new_tile - tile)
            sums[offset] = sums[offset] + both

    earlier = [(ref, slot) for ref, old in zip(spectra, olds) for slot in range(len(old))]
    for new_index in range(len(new)):
        others = [(place, fresh, place) for place in range(new_index + 1)]
        others += [(len(new) + place, ref, slot) for place, (ref, slot) in enumerate(earlier)]
        for first in range(0, len(others), 4):
            meet(new_index, others[first : first + 4])
    if not last:
        out_ref[...] = sums[...]
        return
    real = jnp.concatenate([sums[offset, :, :rows] for offset in range(count)], axis=0)
    imag = jnp.concatenate([sums[offset, :, rows:] for offset in range(count)], axis=0)
    sign = 1.0 - 2.0 * (lax.broadcasted_iota(jnp.int32, real.shape, 1) % 2).astype(jnp.float32)
    none = jnp.zeros((groups, rows), jnp.float32)
    next_real = jnp.concatenate([real[groups:], none], axis=0) * sign
    next_imag = jnp.concatenate([imag[groups:], none], axis=0) * sign
    lags = jnp.dot(
        split(jnp.concatenate([real + next_imag, next_real - imag], axis=1)),
        inverse_ref[...],
        preferred_element_type=jnp.float32,
    )
    squares = jnp.broadcast_to(jnp.sum(lags * lags, keepdims=True), (1, out_ref.shape[2] - groups * rows))
    for offset in range(count):
        sums[offset, :, :rows] = lags[offset * groups : (offset + 1) * groups]
    ways = out_ref.shape[0] // count
    way = lax.axis_index("ch") // inner
    for piece in range(count * ways):
        out_ref[piece, :, groups * rows :] = squares
        out_ref[piece, :, : groups * rows] = jnp.zeros((1, groups * rows), jnp.float32)
    for place in range(count):
        block = sums[lag_ref[place], :, :rows]
        for group in range(groups):
            out_ref[(ways - 1 - way) * count + (count - 1 - place), :, group * rows : (group + 1) * rows] = block[group : group + 1]


def gather_kernel(count, groups, rows, inner, owned_ref, out_ref):
    ways = owned_ref.shape[0] // count
    way = lax.axis_index("ch") // inner
    for place in range(count):
        for group in range(groups):
            row = owned_ref[(ways - 1 - way) * count + (count - 1 - place), :, group * rows : (group + 1) * rows]
            out_ref[place * groups + group : place * groups + group + 1, :] = row


def gather(owned, count, groups, rows, inner):
    vmem = pl.BlockSpec(memory_space=pltpu.VMEM)
    return pl.pallas_call(
        functools.partial(gather_kernel, count, groups, rows, inner),
        out_shape=jax.ShapeDtypeStruct((count * groups, rows), jnp.float32),
        in_specs=[vmem],
        out_specs=vmem,
        compiler_params=pltpu.CompilerParams(vmem_limit_bytes=4 * 2**20),
        cost_estimate=pl.CostEstimate(flops=0, bytes_accessed=count * groups * rows * 8, transcendentals=0),
    )(owned)


def absorb(blocks, new, spectra, olds, carried, tile_order, lag_order, count, ways, inner, last):
    rows, channels = blocks[0].shape[0], blocks[0].shape[1] // 2
    groups = channels // GROUP
    width = math.gcd(rows, 128)
    vmem = pl.BlockSpec(memory_space=pltpu.VMEM)
    anywhere = pl.BlockSpec(memory_space=pl.ANY)
    tables = [jnp.asarray(forward_table(rows))] + ([jnp.asarray(inverse_table(rows))] if last else [])
    operands = tables + list(blocks) + list(spectra) + ([carried] if olds else [])
    out = (count * ways, 1, groups * rows + 128) if last else (count, groups, 2 * rows)
    fresh = jax.ShapeDtypeStruct((len(new), 2 * channels, 2 * rows), jnp.float32)
    result = pl.pallas_call(
        functools.partial(absorb_kernel, count, channels, rows, new, olds, inner, last),
        out_shape=[jax.ShapeDtypeStruct(out, jnp.float32)] + ([] if last else [fresh]),
        in_specs=[anywhere, anywhere] + [vmem] * len(operands),
        out_specs=[vmem] + ([] if last else [vmem]),
        scratch_shapes=([pltpu.VMEM(fresh.shape, jnp.float32)] if last else [])
        + [
            pltpu.VMEM((count, groups, 2 * rows), jnp.float32),
            pltpu.VMEM((rows // width, 2 * channels, width), jnp.float32),
            pltpu.SMEM((count,), jnp.int32),
            pltpu.SMEM((count,), jnp.int32),
            pltpu.SMEM((count,), jnp.int32),
            pltpu.SemaphoreType.DMA((2,)),
        ],
        compiler_params=pltpu.CompilerParams(vmem_limit_bytes=20 * 2**20),
        cost_estimate=pl.CostEstimate(
            flops=24 * len(new) * rows * rows * channels, bytes_accessed=len(new) * rows * channels * 24, transcendentals=0
        ),
    )(tile_order, lag_order, *operands)
    return result[0] if last else result


def shards(inputs, out_grads, tile_order, lag_order):
    count = lax.axis_size("seq")
    rows = inputs.shape[0]
    channels = inputs.shape[1] // count
    groups = channels // GROUP
    ways = lax.axis_size("ch")
    inner = 2 if ways % 2 == 0 else 1
    outer = ways // inner
    half = max(1, count // 2)
    far, near = list(range(count - 1, half - 1, -1)), list(range(half))
    first = cut(inputs, out_grads, count, far[:1])
    inputs, out_grads, first = lax.optimization_barrier((inputs, out_grads, first))
    blocks = dict(zip(far + near, first + cut(inputs, out_grads, count, far[1:] + near)))
    for step in far + near[1:]:
        pairs = [(place, partner(count, place, step)) for place in range(count)]
        blocks[step] = lax.ppermute(blocks[step], "seq", pairs)
    batch = max(1, count // 8)
    early, late = far[:-batch], far[-batch:]
    arrivals = [
        near[:batch] + early[:batch],
        near[batch : 2 * batch] + early[batch : 2 * batch],
        near[2 * batch :],
        early[2 * batch :],
        late,
    ]
    arrivals = [new for new in arrivals if new]
    spectra, olds, carried = [], [], None
    for new in arrivals:
        last = new is arrivals[-1]
        made = absorb(
            [blocks[step] for step in new],
            new,
            spectra,
            list(olds),
            carried,
            tile_order,
            lag_order,
            count,
            outer,
            inner,
            last,
        )
        if not last:
            carried, fresh = made
            spectra.append(fresh)
            olds.append(new)
    together = [
        [place * ways + way * inner + core for way in reversed(range(outer)) for place in reversed(range(count))] for core in range(inner)
    ]
    owned = lax.all_to_all(
        made, ("seq", "ch"), split_axis=0, concat_axis=0, axis_index_groups=together, tiled=True
    )
    squares = owned[:, :, groups * rows :]
    if inner == 2:
        pairs = [(place, place ^ 1) for place in range(ways)]
        squares = squares + lax.ppermute(squares, "ch", pairs)
    total = jnp.sum(squares, axis=(0, 1))
    lags = gather(owned, count, groups, rows, inner)
    entries = ways * count * groups * count * rows
    factor = target_ratio * math.sqrt(entries) / jnp.sqrt(total[:1] + epsilon)
    return lags * factor


def solution(mesh):
    return jax.shard_map(
        shards,
        mesh=mesh,
        in_specs=(P("seq", "ch"), P("seq", "ch"), P(), P()),
        out_specs=P("ch", "seq"),
        check_vma=False,
    )
```

```python
import functools
import math

import jax
import jax.numpy as jnp
import ml_dtypes
import numpy as np
from jax import lax
from jax.experimental import pallas as pl
from jax.experimental.pallas import tpu as pltpu
from jax.sharding import PartitionSpec as P

GROUP = 16
target_ratio = 0.5
epsilon = 1e-12


def halves(table):
    high = table.astype(ml_dtypes.bfloat16)
    low = (table - high.astype(np.float64)).astype(ml_dtypes.bfloat16)
    return np.concatenate([high, high, low], axis=0)


def forward_table(rows):
    angles = np.outer(np.arange(rows), 2 * np.arange(rows) + 1) % (4 * rows) * (math.pi / (2 * rows))
    return halves(np.concatenate([np.cos(angles), -np.sin(angles)], axis=1))


def inverse_table(rows):
    angles = np.outer(2 * np.arange(rows) + 1, np.arange(rows)) % (4 * rows) * (math.pi / (2 * rows))
    return halves(np.concatenate([np.cos(angles), np.sin(angles)], axis=0) / rows)


def split(values):
    high = values.astype(jnp.bfloat16)
    low = (values - high.astype(jnp.float32)).astype(jnp.bfloat16)
    return jnp.concatenate([high, low, high], axis=1)


def partner(count, place, step, back=False):
    if count & (count - 1) == 0:
        return place ^ step
    return (place - step if back else place + step) % count


def cut_kernel(count, channels, steps, inputs_ref, grads_ref, *refs):
    me = lax.axis_index("seq")
    blocks, sems = refs[:-1], refs[-1]
    copies = []
    for index, step in enumerate(steps):
        start = pl.multiple_of(partner(count, me, step) * channels, channels)
        for half, ref in enumerate((inputs_ref, grads_ref)):
            copies.append(
                pltpu.make_async_copy(
                    ref.at[:, pl.ds(start, channels)],
                    blocks[index].at[:, pl.ds(half * channels, channels)],
                    sems.at[2 * index + half],
                )
            )
    for copy in copies:
        copy.start()
    for copy in copies:
        copy.wait()


def cut(inputs, out_grads, count, steps):
    rows, channels = inputs.shape[0], inputs.shape[1] // count
    if channels % 128:
        blocks = []
        for step in steps:
            start = partner(count, lax.axis_index("seq"), step) * channels
            pair = [lax.dynamic_slice_in_dim(whole, start, channels, 1) for whole in (inputs, out_grads)]
            blocks.append(jnp.concatenate(pair, axis=1))
        return blocks
    anywhere = pl.BlockSpec(memory_space=pl.ANY)
    return pl.pallas_call(
        functools.partial(cut_kernel, count, channels, steps),
        out_shape=[jax.ShapeDtypeStruct((rows, 2 * channels), jnp.float32) for _ in steps],
        in_specs=[anywhere, anywhere],
        out_specs=[pl.BlockSpec(memory_space=pltpu.VMEM) for _ in steps],
        scratch_shapes=[pltpu.SemaphoreType.DMA((2 * len(steps),))],
        compiler_params=pltpu.CompilerParams(vmem_limit_bytes=6 * 2**20),
        cost_estimate=pl.CostEstimate(flops=0, bytes_accessed=len(steps) * rows * channels * 16, transcendentals=0),
    )(*(pltpu.with_memory_space_constraint(whole, pltpu.HBM) for whole in (inputs, out_grads)))


def absorb_kernel(count, channels, rows, new, olds, inner, last, order_from, lag_from, forward_ref, *refs):
    refs = list(refs)
    take = lambda many: [refs.pop(0) for _ in range(many)]
    inverse_ref = take(1)[0] if last else None
    blocks, spectra = take(len(new)), take(len(olds))
    carried = take(1)[0] if olds else None
    out_ref = take(1)[0]
    fresh = take(1)[0]
    sums, turned, order_ref, lag_ref, tile_of, sems = take(6)
    width = turned.shape[2]
    scalars = [pltpu.make_async_copy(order_from, order_ref, sems.at[0])]
    if last:
        scalars.append(pltpu.make_async_copy(lag_from, lag_ref, sems.at[1]))
    for copy in scalars:
        copy.start()
    groups = channels // GROUP
    chunk = max(8, groups)

    if carried is None:
        sums[...] = jnp.zeros_like(sums)
    else:
        sums[...] = carried[...]
    for index, step in enumerate(new):
        flipped = blocks[index][...].T
        columns = []
        for part in range(rows // width):
            turned[part] = flipped[:, part * width : (part + 1) * width]
            members = [
                turned[part, pl.ds(half * channels + member, groups, stride=GROUP), :]
                for half in range(2)
                for member in range(GROUP)
            ]
            columns.append(jnp.concatenate(members, axis=0))
        fresh[index] = jnp.dot(
            split(jnp.concatenate(columns, axis=1)), forward_ref[...], preferred_element_type=jnp.float32
        )
    for copy in scalars:
        copy.wait()
    slots = list(new) + [step for old in olds for step in old]
    for index, step in enumerate(slots):
        tile_of[index] = order_ref[partner(count, lax.axis_index("seq"), step, back=True)]

    def meet(new_index, others):
        new_tile = tile_of[new_index]
        tiles = [tile_of[place] for place, _, _ in others]
        later = [jnp.full((chunk, rows), (new_tile > tile).astype(jnp.int32)) > 0 for tile in tiles]
        bases = [jnp.where(new_tile > tile, 0, channels) for tile in tiles]

        def step(index, totals):
            start = index * chunk
            input_rows = slice(start, start + chunk)
            grad_rows = slice(channels + start, channels + start + chunk)
            input_real, input_imag = fresh[new_index, input_rows, :rows], fresh[new_index, input_rows, rows:]
            grad_real, grad_imag = fresh[new_index, grad_rows, :rows], fresh[new_index, grad_rows, rows:]
            out = []
            for (_, ref, slot), is_later, base, (total_real, total_imag) in zip(others, later, bases, totals):
                its_rows = pl.ds(pl.multiple_of(base + start, chunk), chunk)
                real, imag = ref[slot, its_rows, :rows], ref[slot, its_rows, rows:]
                new_real = jnp.where(is_later, grad_real, input_real)
                new_imag = jnp.where(is_later, grad_imag, input_imag)
                out.append(
                    (
                        total_real + (new_real * real + new_imag * imag),
                        total_imag + (new_real * imag - new_imag * real),
                    )
                )
            return out

        zero = jnp.zeros((chunk, rows), jnp.float32)
        totals = [(zero, zero) for _ in others]
        for index in range(channels // chunk):
            totals = step(index, totals)
        for tile, (total_real, total_imag) in zip(tiles, totals):
            total_imag = total_imag * jnp.where(new_tile > tile, -1.0, 1.0)
            both = jnp.concatenate([total_real, total_imag], axis=1)
            if chunk > groups:
                both = sum(both[row : row + groups] for row in range(0, chunk, groups))
            offset = jnp.abs(new_tile - tile)
            sums[offset] = sums[offset] + both

    earlier = [(ref, slot) for ref, old in zip(spectra, olds) for slot in range(len(old))]
    for new_index in range(len(new)):
        others = [(place, fresh, place) for place in range(new_index + 1)]
        others += [(len(new) + place, ref, slot) for place, (ref, slot) in enumerate(earlier)]
        for first in range(0, len(others), 4):
            meet(new_index, others[first : first + 4])
    if not last:
        out_ref[...] = sums[...]
        return
    real = jnp.concatenate([sums[offset, :, :rows] for offset in range(count)], axis=0)
    imag = jnp.concatenate([sums[offset, :, rows:] for offset in range(count)], axis=0)
    sign = 1.0 - 2.0 * (lax.broadcasted_iota(jnp.int32, real.shape, 1) % 2).astype(jnp.float32)
    none = jnp.zeros((groups, rows), jnp.float32)
    next_real = jnp.concatenate([real[groups:], none], axis=0) * sign
    next_imag = jnp.concatenate([imag[groups:], none], axis=0) * sign
    lags = jnp.dot(
        split(jnp.concatenate([real + next_imag, next_real - imag], axis=1)),
        inverse_ref[...],
        preferred_element_type=jnp.float32,
    )
    squares = jnp.broadcast_to(jnp.sum(lags * lags, keepdims=True), (1, out_ref.shape[2] - groups * rows))
    for offset in range(count):
        sums[offset, :, :rows] = lags[offset * groups : (offset + 1) * groups]
    ways = out_ref.shape[0] // count
    way = lax.axis_index("ch") // inner
    for piece in range(count * ways):
        out_ref[piece, :, groups * rows :] = squares
        out_ref[piece, :, : groups * rows] = jnp.zeros((1, groups * rows), jnp.float32)
    for place in range(count):
        block = sums[lag_ref[place], :, :rows]
        for group in range(groups):
            piece = (ways - 1 - way) * count + (count - 1 - place)
            out_ref[piece, :, group * rows : (group + 1) * rows] = block[group : group + 1]


def gather_kernel(count, groups, rows, inner, owned_ref, out_ref):
    ways = owned_ref.shape[0] // count
    way = lax.axis_index("ch") // inner
    for place in range(count):
        for group in range(groups):
            row = owned_ref[(ways - 1 - way) * count + (count - 1 - place), :, group * rows : (group + 1) * rows]
            out_ref[place * groups + group : place * groups + group + 1, :] = row


def gather(owned, count, groups, rows, inner):
    vmem = pl.BlockSpec(memory_space=pltpu.VMEM)
    return pl.pallas_call(
        functools.partial(gather_kernel, count, groups, rows, inner),
        out_shape=jax.ShapeDtypeStruct((count * groups, rows), jnp.float32),
        in_specs=[vmem],
        out_specs=vmem,
        compiler_params=pltpu.CompilerParams(vmem_limit_bytes=4 * 2**20),
        cost_estimate=pl.CostEstimate(flops=0, bytes_accessed=count * groups * rows * 8, transcendentals=0),
    )(owned)


def absorb(blocks, new, spectra, olds, carried, tile_order, lag_order, count, ways, inner, last):
    rows, channels = blocks[0].shape[0], blocks[0].shape[1] // 2
    groups = channels // GROUP
    width = math.gcd(rows, 128)
    vmem = pl.BlockSpec(memory_space=pltpu.VMEM)
    anywhere = pl.BlockSpec(memory_space=pl.ANY)
    tables = [jnp.asarray(forward_table(rows))] + ([jnp.asarray(inverse_table(rows))] if last else [])
    operands = tables + list(blocks) + list(spectra) + ([carried] if olds else [])
    out = (count * ways, 1, groups * rows + 128) if last else (count, groups, 2 * rows)
    fresh = jax.ShapeDtypeStruct((len(new), 2 * channels, 2 * rows), jnp.float32)
    result = pl.pallas_call(
        functools.partial(absorb_kernel, count, channels, rows, new, olds, inner, last),
        out_shape=[jax.ShapeDtypeStruct(out, jnp.float32)] + ([] if last else [fresh]),
        in_specs=[anywhere, anywhere] + [vmem] * len(operands),
        out_specs=[vmem] + ([] if last else [vmem]),
        scratch_shapes=([pltpu.VMEM(fresh.shape, jnp.float32)] if last else [])
        + [
            pltpu.VMEM((count, groups, 2 * rows), jnp.float32),
            pltpu.VMEM((rows // width, 2 * channels, width), jnp.float32),
            pltpu.SMEM((count,), jnp.int32),
            pltpu.SMEM((count,), jnp.int32),
            pltpu.SMEM((count,), jnp.int32),
            pltpu.SemaphoreType.DMA((2,)),
        ],
        compiler_params=pltpu.CompilerParams(vmem_limit_bytes=20 * 2**20),
        cost_estimate=pl.CostEstimate(
            flops=24 * len(new) * rows * rows * channels, bytes_accessed=len(new) * rows * channels * 24, transcendentals=0
        ),
    )(tile_order, lag_order, *operands)
    return result[0] if last else result


def shards(inputs, out_grads, tile_order, lag_order):
    count = lax.axis_size("seq")
    rows = inputs.shape[0]
    channels = inputs.shape[1] // count
    groups = channels // GROUP
    ways = lax.axis_size("ch")
    inner = 2 if ways % 2 == 0 else 1
    outer = ways // inner
    half = max(1, count // 2)
    middle, wide = half // 2, count - half
    far = [half + step for step in dict.fromkeys([wide // 2, *range(1, wide), 0])]
    near = list(dict.fromkeys([0, *(step for step in range(1, half) if step != middle), middle]))
    first = cut(inputs, out_grads, count, far[:1])
    inputs, out_grads, first = lax.optimization_barrier((inputs, out_grads, first))
    blocks = dict(zip(far + near, first + cut(inputs, out_grads, count, far[1:] + near)))
    for step in far + near[1:]:
        pairs = [(place, partner(count, place, step)) for place in range(count)]
        blocks[step] = lax.ppermute(blocks[step], "seq", pairs)
    batch = max(1, count // 8)
    early, late = far[:-batch], far[-batch:]
    arrivals = [
        near[:batch] + early[:batch],
        near[batch : 2 * batch] + early[batch : 2 * batch],
        near[2 * batch :],
        early[2 * batch :],
        late,
    ]
    arrivals = [new for new in arrivals if new]
    spectra, olds, carried = [], [], None
    for new in arrivals:
        last = new is arrivals[-1]
        made = absorb(
            [blocks[step] for step in new],
            new,
            spectra,
            list(olds),
            carried,
            tile_order,
            lag_order,
            count,
            outer,
            inner,
            last,
        )
        if not last:
            carried, fresh = made
            spectra.append(fresh)
            olds.append(new)
    together = [
        [place * ways + way * inner + core for way in reversed(range(outer)) for place in reversed(range(count))]
        for core in range(inner)
    ]
    owned = lax.all_to_all(
        made, ("seq", "ch"), split_axis=0, concat_axis=0, axis_index_groups=together, tiled=True
    )
    squares = owned[:, :, groups * rows :]
    if inner == 2:
        pairs = [(place, place ^ 1) for place in range(ways)]
        squares = squares + lax.ppermute(squares, "ch", pairs)
    total = jnp.sum(squares, axis=(0, 1))
    lags = gather(owned, count, groups, rows, inner)
    entries = ways * count * groups * count * rows
    factor = target_ratio * math.sqrt(entries) / jnp.sqrt(total[:1] + epsilon)
    return lags * factor


def solution(mesh):
    return jax.shard_map(
        shards,
        mesh=mesh,
        in_specs=(P("seq", "ch"), P("seq", "ch"), P(), P()),
        out_specs=P("ch", "seq"),
        check_vma=False,
    )
```

```python
import functools
import math

import jax
import jax.numpy as jnp
import ml_dtypes
import numpy as np
from jax import lax
from jax.experimental import pallas as pl
from jax.experimental.pallas import tpu as pltpu
from jax.sharding import PartitionSpec as P

GROUP = 16
target_ratio = 0.5
epsilon = 1e-12


def halves(table):
    high = table.astype(ml_dtypes.bfloat16)
    low = (table - high.astype(np.float64)).astype(ml_dtypes.bfloat16)
    return np.concatenate([high, high, low], axis=0)


def forward_table(rows):
    angles = np.outer(np.arange(rows), 2 * np.arange(rows) + 1) % (4 * rows) * (math.pi / (2 * rows))
    return halves(np.concatenate([np.cos(angles), -np.sin(angles)], axis=1))


def inverse_table(rows):
    angles = np.outer(2 * np.arange(rows) + 1, np.arange(rows)) % (4 * rows) * (math.pi / (2 * rows))
    return halves(np.concatenate([np.cos(angles), np.sin(angles)], axis=0) / rows)


def split(values):
    high = values.astype(jnp.bfloat16)
    low = (values - high.astype(jnp.float32)).astype(jnp.bfloat16)
    return jnp.concatenate([high, low, high], axis=1)


def partner(count, place, step, back=False):
    if count & (count - 1) == 0:
        return place ^ step
    return (place - step if back else place + step) % count


def turns(count):
    quarter = max(1, count // 4)
    quarters = [list(range(first, min(first + quarter, count)))[::-1] for first in range(0, count, quarter)]
    middle = quarters[1:-1][::-1]
    return [place for part in middle + quarters[:0:-1][:1] + quarters[:1] for place in part]


def cut_kernel(count, channels, steps, inputs_ref, grads_ref, *refs):
    me = lax.axis_index("seq")
    blocks, sems = refs[:-1], refs[-1]
    copies = []
    for index, step in enumerate(steps):
        start = pl.multiple_of(partner(count, me, step) * channels, channels)
        for half, ref in enumerate((inputs_ref, grads_ref)):
            copies.append(
                pltpu.make_async_copy(
                    ref.at[:, pl.ds(start, channels)],
                    blocks[index].at[:, pl.ds(half * channels, channels)],
                    sems.at[2 * index + half],
                )
            )
    for copy in copies:
        copy.start()
    for copy in copies:
        copy.wait()


def cut(inputs, out_grads, count, steps):
    rows, channels = inputs.shape[0], inputs.shape[1] // count
    if channels % 128:
        blocks = []
        for step in steps:
            start = partner(count, lax.axis_index("seq"), step) * channels
            pair = [lax.dynamic_slice_in_dim(whole, start, channels, 1) for whole in (inputs, out_grads)]
            blocks.append(jnp.concatenate(pair, axis=1))
        return blocks
    anywhere = pl.BlockSpec(memory_space=pl.ANY)
    return pl.pallas_call(
        functools.partial(cut_kernel, count, channels, steps),
        out_shape=[jax.ShapeDtypeStruct((rows, 2 * channels), jnp.float32) for _ in steps],
        in_specs=[anywhere, anywhere],
        out_specs=[pl.BlockSpec(memory_space=pltpu.VMEM) for _ in steps],
        scratch_shapes=[pltpu.SemaphoreType.DMA((2 * len(steps),))],
        compiler_params=pltpu.CompilerParams(vmem_limit_bytes=6 * 2**20),
        cost_estimate=pl.CostEstimate(flops=0, bytes_accessed=len(steps) * rows * channels * 16, transcendentals=0),
    )(*(pltpu.with_memory_space_constraint(whole, pltpu.HBM) for whole in (inputs, out_grads)))


def absorb_kernel(count, channels, rows, new, olds, inner, last, order_from, lag_from, forward_ref, *refs):
    refs = list(refs)
    take = lambda many: [refs.pop(0) for _ in range(many)]
    inverse_ref = take(1)[0] if last else None
    blocks, spectra = take(len(new)), take(len(olds))
    carried = take(1)[0] if olds else None
    out_ref = take(1)[0]
    fresh = take(1)[0]
    sums, turned, order_ref, lag_ref, tile_of, sems = take(6)
    width = turned.shape[2]
    scalars = [pltpu.make_async_copy(order_from, order_ref, sems.at[0])]
    if last:
        scalars.append(pltpu.make_async_copy(lag_from, lag_ref, sems.at[1]))
    for copy in scalars:
        copy.start()
    groups = channels // GROUP
    chunk = max(8, groups)

    if carried is None:
        sums[...] = jnp.zeros_like(sums)
    else:
        sums[...] = carried[...]
    for index, step in enumerate(new):
        flipped = blocks[index][...].T
        columns = []
        for part in range(rows // width):
            turned[part] = flipped[:, part * width : (part + 1) * width]
            members = [
                turned[part, pl.ds(half * channels + member, groups, stride=GROUP), :]
                for half in range(2)
                for member in range(GROUP)
            ]
            columns.append(jnp.concatenate(members, axis=0))
        fresh[index] = jnp.dot(
            split(jnp.concatenate(columns, axis=1)), forward_ref[...], preferred_element_type=jnp.float32
        )
    for copy in scalars:
        copy.wait()
    slots = list(new) + [step for old in olds for step in old]
    for index, step in enumerate(slots):
        tile_of[index] = order_ref[partner(count, lax.axis_index("seq"), step, back=True)]

    def meet(new_index, others):
        new_tile = tile_of[new_index]
        tiles = [tile_of[place] for place, _, _ in others]
        later = [jnp.full((chunk, rows), (new_tile > tile).astype(jnp.int32)) > 0 for tile in tiles]
        bases = [jnp.where(new_tile > tile, 0, channels) for tile in tiles]

        def step(index, totals):
            start = index * chunk
            input_rows = slice(start, start + chunk)
            grad_rows = slice(channels + start, channels + start + chunk)
            input_real, input_imag = fresh[new_index, input_rows, :rows], fresh[new_index, input_rows, rows:]
            grad_real, grad_imag = fresh[new_index, grad_rows, :rows], fresh[new_index, grad_rows, rows:]
            out = []
            for (_, ref, slot), is_later, base, (total_real, total_imag) in zip(others, later, bases, totals):
                its_rows = pl.ds(pl.multiple_of(base + start, chunk), chunk)
                real, imag = ref[slot, its_rows, :rows], ref[slot, its_rows, rows:]
                new_real = jnp.where(is_later, grad_real, input_real)
                new_imag = jnp.where(is_later, grad_imag, input_imag)
                out.append(
                    (
                        total_real + (new_real * real + new_imag * imag),
                        total_imag + (new_real * imag - new_imag * real),
                    )
                )
            return out

        zero = jnp.zeros((chunk, rows), jnp.float32)
        totals = [(zero, zero) for _ in others]
        for index in range(channels // chunk):
            totals = step(index, totals)
        for tile, (total_real, total_imag) in zip(tiles, totals):
            total_imag = total_imag * jnp.where(new_tile > tile, -1.0, 1.0)
            both = jnp.concatenate([total_real, total_imag], axis=1)
            if chunk > groups:
                both = sum(both[row : row + groups] for row in range(0, chunk, groups))
            offset = jnp.abs(new_tile - tile)
            sums[offset] = sums[offset] + both

    earlier = [(ref, slot) for ref, old in zip(spectra, olds) for slot in range(len(old))]
    for new_index in range(len(new)):
        others = [(place, fresh, place) for place in range(new_index + 1)]
        others += [(len(new) + place, ref, slot) for place, (ref, slot) in enumerate(earlier)]
        for first in range(0, len(others), 4):
            meet(new_index, others[first : first + 4])
    if not last:
        out_ref[...] = sums[...]
        return
    real = jnp.concatenate([sums[offset, :, :rows] for offset in range(count)], axis=0)
    imag = jnp.concatenate([sums[offset, :, rows:] for offset in range(count)], axis=0)
    sign = 1.0 - 2.0 * (lax.broadcasted_iota(jnp.int32, real.shape, 1) % 2).astype(jnp.float32)
    none = jnp.zeros((groups, rows), jnp.float32)
    next_real = jnp.concatenate([real[groups:], none], axis=0) * sign
    next_imag = jnp.concatenate([imag[groups:], none], axis=0) * sign
    lags = jnp.dot(
        split(jnp.concatenate([real + next_imag, next_real - imag], axis=1)),
        inverse_ref[...],
        preferred_element_type=jnp.float32,
    )
    squares = jnp.broadcast_to(jnp.sum(lags * lags, keepdims=True), (1, out_ref.shape[2] - groups * rows))
    for offset in range(count):
        sums[offset, :, :rows] = lags[offset * groups : (offset + 1) * groups]
    ways = out_ref.shape[0] // count
    way = lax.axis_index("ch") // inner
    for piece in range(count * ways):
        out_ref[piece, :, groups * rows :] = squares
        out_ref[piece, :, : groups * rows] = jnp.zeros((1, groups * rows), jnp.float32)
    for place in range(count):
        block = sums[lag_ref[place], :, :rows]
        for group in range(groups):
            piece = turns(count).index(place) * ways + ways - 1 - way
            out_ref[piece, :, group * rows : (group + 1) * rows] = block[group : group + 1]


def gather_kernel(count, groups, rows, inner, owned_ref, out_ref):
    ways = owned_ref.shape[0] // count
    way = lax.axis_index("ch") // inner
    for place in range(count):
        for group in range(groups):
            row = owned_ref[turns(count).index(place) * ways + ways - 1 - way, :, group * rows : (group + 1) * rows]
            out_ref[place * groups + group : place * groups + group + 1, :] = row


def gather(owned, count, groups, rows, inner):
    vmem = pl.BlockSpec(memory_space=pltpu.VMEM)
    return pl.pallas_call(
        functools.partial(gather_kernel, count, groups, rows, inner),
        out_shape=jax.ShapeDtypeStruct((count * groups, rows), jnp.float32),
        in_specs=[vmem],
        out_specs=vmem,
        compiler_params=pltpu.CompilerParams(vmem_limit_bytes=4 * 2**20),
        cost_estimate=pl.CostEstimate(flops=0, bytes_accessed=count * groups * rows * 8, transcendentals=0),
    )(owned)


def absorb(blocks, new, spectra, olds, carried, tile_order, lag_order, count, ways, inner, last):
    rows, channels = blocks[0].shape[0], blocks[0].shape[1] // 2
    groups = channels // GROUP
    width = math.gcd(rows, 128)
    vmem = pl.BlockSpec(memory_space=pltpu.VMEM)
    anywhere = pl.BlockSpec(memory_space=pl.ANY)
    tables = [jnp.asarray(forward_table(rows))] + ([jnp.asarray(inverse_table(rows))] if last else [])
    operands = tables + list(blocks) + list(spectra) + ([carried] if olds else [])
    out = (count * ways, 1, groups * rows + 128) if last else (count, groups, 2 * rows)
    fresh = jax.ShapeDtypeStruct((len(new), 2 * channels, 2 * rows), jnp.float32)
    result = pl.pallas_call(
        functools.partial(absorb_kernel, count, channels, rows, new, olds, inner, last),
        out_shape=[jax.ShapeDtypeStruct(out, jnp.float32)] + ([] if last else [fresh]),
        in_specs=[anywhere, anywhere] + [vmem] * len(operands),
        out_specs=[vmem] + ([] if last else [vmem]),
        scratch_shapes=([pltpu.VMEM(fresh.shape, jnp.float32)] if last else [])
        + [
            pltpu.VMEM((count, groups, 2 * rows), jnp.float32),
            pltpu.VMEM((rows // width, 2 * channels, width), jnp.float32),
            pltpu.SMEM((count,), jnp.int32),
            pltpu.SMEM((count,), jnp.int32),
            pltpu.SMEM((count,), jnp.int32),
            pltpu.SemaphoreType.DMA((2,)),
        ],
        compiler_params=pltpu.CompilerParams(vmem_limit_bytes=20 * 2**20),
        cost_estimate=pl.CostEstimate(
            flops=24 * len(new) * rows * rows * channels, bytes_accessed=len(new) * rows * channels * 24, transcendentals=0
        ),
    )(tile_order, lag_order, *operands)
    return result[0] if last else result


def shards(inputs, out_grads, tile_order, lag_order):
    count = lax.axis_size("seq")
    rows = inputs.shape[0]
    channels = inputs.shape[1] // count
    groups = channels // GROUP
    ways = lax.axis_size("ch")
    inner = 2 if ways % 2 == 0 else 1
    outer = ways // inner
    half = max(1, count // 2)
    middle, wide = half // 2, count - half
    far = [half + step for step in dict.fromkeys([wide // 2, *range(1, wide), 0])]
    near = list(dict.fromkeys([0, *(step for step in range(1, half) if step != middle), middle]))
    first = cut(inputs, out_grads, count, far[:1])
    inputs, out_grads, first = lax.optimization_barrier((inputs, out_grads, first))
    blocks = dict(zip(far + near, first + cut(inputs, out_grads, count, far[1:] + near)))
    for step in far + near[1:]:
        pairs = [(place, partner(count, place, step)) for place in range(count)]
        blocks[step] = lax.ppermute(blocks[step], "seq", pairs)
    batch = max(1, count // 8)
    early, late = far[:-batch], far[-batch:]
    arrivals = [
        near[:batch] + early[:batch],
        near[batch : 2 * batch] + early[batch : 2 * batch],
        near[2 * batch :],
        early[2 * batch :],
        late,
    ]
    arrivals = [new for new in arrivals if new]
    spectra, olds, carried = [], [], None
    for new in arrivals:
        last = new is arrivals[-1]
        made = absorb(
            [blocks[step] for step in new],
            new,
            spectra,
            list(olds),
            carried,
            tile_order,
            lag_order,
            count,
            outer,
            inner,
            last,
        )
        if not last:
            carried, fresh = made
            spectra.append(fresh)
            olds.append(new)
    together = [
        [place * ways + way * inner + core for place in turns(count) for way in reversed(range(outer))]
        for core in range(inner)
    ]
    owned = lax.all_to_all(
        made, ("seq", "ch"), split_axis=0, concat_axis=0, axis_index_groups=together, tiled=True
    )
    squares = owned[:, :, groups * rows :]
    if inner == 2:
        pairs = [(place, place ^ 1) for place in range(ways)]
        squares = squares + lax.ppermute(squares, "ch", pairs)
    total = jnp.sum(squares, axis=(0, 1))
    lags = gather(owned, count, groups, rows, inner)
    entries = ways * count * groups * count * rows
    factor = target_ratio * math.sqrt(entries) / jnp.sqrt(total[:1] + epsilon)
    return lags * factor


def solution(mesh):
    return jax.shard_map(
        shards,
        mesh=mesh,
        in_specs=(P("seq", "ch"), P("seq", "ch"), P(), P()),
        out_specs=P("ch", "seq"),
        check_vma=False,
    )
```

```python
import functools
import math

import jax
import jax.numpy as jnp
import ml_dtypes
import numpy as np
from jax import lax
from jax.experimental import pallas as pl
from jax.experimental.pallas import tpu as pltpu
from jax.sharding import PartitionSpec as P

GROUP = 16
target_ratio = 0.5
epsilon = 1e-12


def halves(table):
    high = table.astype(ml_dtypes.bfloat16)
    low = (table - high.astype(np.float64)).astype(ml_dtypes.bfloat16)
    return np.concatenate([high, high, low], axis=0)


def forward_table(rows):
    angles = np.outer(np.arange(rows), 2 * np.arange(rows) + 1) % (4 * rows) * (math.pi / (2 * rows))
    return halves(np.concatenate([np.cos(angles), -np.sin(angles)], axis=1))


def inverse_table(rows):
    angles = np.outer(2 * np.arange(rows) + 1, np.arange(rows)) % (4 * rows) * (math.pi / (2 * rows))
    return halves(np.concatenate([np.cos(angles), np.sin(angles)], axis=0) / rows)


def split(values):
    high = values.astype(jnp.bfloat16)
    low = (values - high.astype(jnp.float32)).astype(jnp.bfloat16)
    return jnp.concatenate([high, low, high], axis=1)


def partner(count, place, step, back=False):
    if count & (count - 1) == 0:
        return place ^ step
    return (place - step if back else place + step) % count


def turns(count):
    quarter = max(1, count // 4)
    quarters = [list(range(first, min(first + quarter, count)))[::-1] for first in range(0, count, quarter)]
    middle = quarters[1:-1][::-1]
    return [place for part in middle + quarters[:0:-1][:1] + quarters[:1] for place in part]


def cut_kernel(count, channels, steps, inputs_ref, grads_ref, *refs):
    me = lax.axis_index("seq")
    blocks, sems = refs[:-1], refs[-1]
    copies = []
    for index, step in enumerate(steps):
        start = pl.multiple_of(partner(count, me, step) * channels, channels)
        for half, ref in enumerate((inputs_ref, grads_ref)):
            copies.append(
                pltpu.make_async_copy(
                    ref.at[:, pl.ds(start, channels)],
                    blocks[index].at[:, pl.ds(half * channels, channels)],
                    sems.at[2 * index + half],
                )
            )
    for copy in copies:
        copy.start()
    for copy in copies:
        copy.wait()


def cut(inputs, out_grads, count, steps):
    rows, channels = inputs.shape[0], inputs.shape[1] // count
    if channels % 128:
        blocks = []
        for step in steps:
            start = partner(count, lax.axis_index("seq"), step) * channels
            pair = [lax.dynamic_slice_in_dim(whole, start, channels, 1) for whole in (inputs, out_grads)]
            blocks.append(jnp.concatenate(pair, axis=1))
        return blocks
    anywhere = pl.BlockSpec(memory_space=pl.ANY)
    return pl.pallas_call(
        functools.partial(cut_kernel, count, channels, steps),
        out_shape=[jax.ShapeDtypeStruct((rows, 2 * channels), jnp.float32) for _ in steps],
        in_specs=[anywhere, anywhere],
        out_specs=[pl.BlockSpec(memory_space=pltpu.VMEM) for _ in steps],
        scratch_shapes=[pltpu.SemaphoreType.DMA((2 * len(steps),))],
        compiler_params=pltpu.CompilerParams(vmem_limit_bytes=6 * 2**20),
        cost_estimate=pl.CostEstimate(flops=0, bytes_accessed=len(steps) * rows * channels * 16, transcendentals=0),
    )(*(pltpu.with_memory_space_constraint(whole, pltpu.HBM) for whole in (inputs, out_grads)))


def absorb_kernel(count, channels, rows, new, olds, inner, last, order_from, lag_from, forward_ref, *refs):
    refs = list(refs)
    take = lambda many: [refs.pop(0) for _ in range(many)]
    inverse_ref = take(1)[0] if last else None
    blocks, spectra = take(len(new)), take(len(olds))
    carried = take(1)[0] if olds else None
    out_ref = take(1)[0]
    fresh = take(1)[0]
    sums, turned, order_ref, lag_ref, tile_of, sems = take(6)
    width = turned.shape[2]
    scalars = [pltpu.make_async_copy(order_from, order_ref, sems.at[0])]
    if last:
        scalars.append(pltpu.make_async_copy(lag_from, lag_ref, sems.at[1]))
    for copy in scalars:
        copy.start()
    groups = channels // GROUP
    chunk = max(8, groups)

    if carried is None:
        sums[...] = jnp.zeros_like(sums)
    else:
        sums[...] = carried[...]
    for index, step in enumerate(new):
        flipped = blocks[index][...].T
        columns = []
        for part in range(rows // width):
            turned[part] = flipped[:, part * width : (part + 1) * width]
            members = [
                turned[part, pl.ds(half * channels + member, groups, stride=GROUP), :]
                for half in range(2)
                for member in range(GROUP)
            ]
            columns.append(jnp.concatenate(members, axis=0))
        fresh[index] = jnp.dot(
            split(jnp.concatenate(columns, axis=1)), forward_ref[...], preferred_element_type=jnp.float32
        )
    for copy in scalars:
        copy.wait()
    slots = list(new) + [step for old in olds for step in old]
    for index, step in enumerate(slots):
        tile_of[index] = order_ref[partner(count, lax.axis_index("seq"), step, back=True)]

    def meet(new_index, others):
        new_tile = tile_of[new_index]
        tiles = [tile_of[place] for place, _, _ in others]
        later = [jnp.full((chunk, rows), (new_tile > tile).astype(jnp.int32)) > 0 for tile in tiles]
        bases = [jnp.where(new_tile > tile, 0, channels) for tile in tiles]

        def step(index, totals):
            start = index * chunk
            input_rows = slice(start, start + chunk)
            grad_rows = slice(channels + start, channels + start + chunk)
            input_real, input_imag = fresh[new_index, input_rows, :rows], fresh[new_index, input_rows, rows:]
            grad_real, grad_imag = fresh[new_index, grad_rows, :rows], fresh[new_index, grad_rows, rows:]
            out = []
            for (_, ref, slot), is_later, base, (total_real, total_imag) in zip(others, later, bases, totals):
                its_rows = pl.ds(pl.multiple_of(base + start, chunk), chunk)
                real, imag = ref[slot, its_rows, :rows], ref[slot, its_rows, rows:]
                new_real = jnp.where(is_later, grad_real, input_real)
                new_imag = jnp.where(is_later, grad_imag, input_imag)
                out.append(
                    (
                        total_real + (new_real * real + new_imag * imag),
                        total_imag + (new_real * imag - new_imag * real),
                    )
                )
            return out

        zero = jnp.zeros((chunk, rows), jnp.float32)
        totals = [(zero, zero) for _ in others]
        for index in range(channels // chunk):
            totals = step(index, totals)
        for tile, (total_real, total_imag) in zip(tiles, totals):
            total_imag = total_imag * jnp.where(new_tile > tile, -1.0, 1.0)
            both = jnp.concatenate([total_real, total_imag], axis=1)
            if chunk > groups:
                both = sum(both[row : row + groups] for row in range(0, chunk, groups))
            offset = jnp.abs(new_tile - tile)
            sums[offset] = sums[offset] + both

    earlier = [(ref, slot) for ref, old in zip(spectra, olds) for slot in range(len(old))]
    for new_index in range(len(new)):
        others = [(place, fresh, place) for place in range(new_index + 1)]
        others += [(len(new) + place, ref, slot) for place, (ref, slot) in enumerate(earlier)]
        for first in range(0, len(others), 4):
            meet(new_index, others[first : first + 4])
    if not last:
        out_ref[...] = sums[...]
        return
    real = jnp.concatenate([sums[offset, :, :rows] for offset in range(count)], axis=0)
    imag = jnp.concatenate([sums[offset, :, rows:] for offset in range(count)], axis=0)
    sign = 1.0 - 2.0 * (lax.broadcasted_iota(jnp.int32, real.shape, 1) % 2).astype(jnp.float32)
    none = jnp.zeros((groups, rows), jnp.float32)
    next_real = jnp.concatenate([real[groups:], none], axis=0) * sign
    next_imag = jnp.concatenate([imag[groups:], none], axis=0) * sign
    lags = jnp.dot(
        split(jnp.concatenate([real + next_imag, next_real - imag], axis=1)),
        inverse_ref[...],
        preferred_element_type=jnp.float32,
    )
    squares = jnp.broadcast_to(jnp.sum(lags * lags, keepdims=True), (1, out_ref.shape[2] - groups * rows))
    for offset in range(count):
        sums[offset, :, :rows] = lags[offset * groups : (offset + 1) * groups]
    ways = out_ref.shape[0] // count
    way = lax.axis_index("ch") // inner
    for piece in range(count * ways):
        out_ref[piece, :, groups * rows :] = squares
        out_ref[piece, :, : groups * rows] = jnp.zeros((1, groups * rows), jnp.float32)
    for place in range(count):
        block = sums[lag_ref[place], :, :rows]
        for group in range(groups):
            piece = turns(count).index(place) * ways + ways - 1 - way
            out_ref[piece, :, group * rows : (group + 1) * rows] = block[group : group + 1]


def gather_kernel(count, groups, rows, inner, owned_ref, out_ref):
    ways = owned_ref.shape[0] // count
    way = lax.axis_index("ch") // inner
    for place in range(count):
        for group in range(groups):
            row = owned_ref[turns(count).index(place) * ways + ways - 1 - way, :, group * rows : (group + 1) * rows]
            out_ref[place * groups + group : place * groups + group + 1, :] = row


def gather(owned, count, groups, rows, inner):
    vmem = pl.BlockSpec(memory_space=pltpu.VMEM)
    return pl.pallas_call(
        functools.partial(gather_kernel, count, groups, rows, inner),
        out_shape=jax.ShapeDtypeStruct((count * groups, rows), jnp.float32),
        in_specs=[vmem],
        out_specs=vmem,
        compiler_params=pltpu.CompilerParams(vmem_limit_bytes=4 * 2**20),
        cost_estimate=pl.CostEstimate(flops=0, bytes_accessed=count * groups * rows * 8, transcendentals=0),
    )(owned)


def absorb(blocks, new, spectra, olds, carried, tile_order, lag_order, count, ways, inner, last):
    rows, channels = blocks[0].shape[0], blocks[0].shape[1] // 2
    groups = channels // GROUP
    width = math.gcd(rows, 128)
    vmem = pl.BlockSpec(memory_space=pltpu.VMEM)
    anywhere = pl.BlockSpec(memory_space=pl.ANY)
    tables = [jnp.asarray(forward_table(rows))] + ([jnp.asarray(inverse_table(rows))] if last else [])
    operands = tables + list(blocks) + list(spectra) + ([carried] if olds else [])
    out = (count * ways, 1, groups * rows + 128) if last else (count, groups, 2 * rows)
    fresh = jax.ShapeDtypeStruct((len(new), 2 * channels, 2 * rows), jnp.float32)
    result = pl.pallas_call(
        functools.partial(absorb_kernel, count, channels, rows, new, olds, inner, last),
        out_shape=[jax.ShapeDtypeStruct(out, jnp.float32)] + ([] if last else [fresh]),
        in_specs=[anywhere, anywhere] + [vmem] * len(operands),
        out_specs=[vmem] + ([] if last else [vmem]),
        scratch_shapes=([pltpu.VMEM(fresh.shape, jnp.float32)] if last else [])
        + [
            pltpu.VMEM((count, groups, 2 * rows), jnp.float32),
            pltpu.VMEM((rows // width, 2 * channels, width), jnp.float32),
            pltpu.SMEM((count,), jnp.int32),
            pltpu.SMEM((count,), jnp.int32),
            pltpu.SMEM((count,), jnp.int32),
            pltpu.SemaphoreType.DMA((2,)),
        ],
        compiler_params=pltpu.CompilerParams(vmem_limit_bytes=20 * 2**20),
        cost_estimate=pl.CostEstimate(
            flops=24 * len(new) * rows * rows * channels, bytes_accessed=len(new) * rows * channels * 24, transcendentals=0
        ),
    )(tile_order, lag_order, *operands)
    return result[0] if last else result


def shards(inputs, out_grads, tile_order, lag_order):
    count = lax.axis_size("seq")
    rows = inputs.shape[0]
    channels = inputs.shape[1] // count
    groups = channels // GROUP
    ways = lax.axis_size("ch")
    inner = 2 if ways % 2 == 0 else 1
    outer = ways // inner
    half = max(1, count // 2)
    middle, wide = half // 2, count - half
    far = [half + step for step in dict.fromkeys([wide // 2, *range(1, wide), 0])]
    near = list(dict.fromkeys([0, *(step for step in range(1, half) if step != middle), middle]))
    def exchange(step, block):
        return lax.ppermute(block, "seq", [(place, partner(count, place, step)) for place in range(count)])

    start = partner(count, lax.axis_index("seq"), far[0]) * channels
    halves_of_first = [lax.dynamic_slice_in_dim(whole, start, channels, 1) for whole in (inputs, out_grads)]
    blocks = dict(zip(far[1:] + near, cut(inputs, out_grads, count, far[1:] + near)))
    blocks[far[0]] = jnp.concatenate([exchange(far[0], part) for part in halves_of_first], axis=1)
    for step in far[1:] + near[1:]:
        blocks[step] = exchange(step, blocks[step])
    batch = max(1, count // 8)
    early, late = far[:-batch], far[-batch:]
    arrivals = [
        near[:batch] + early[:batch],
        near[batch : 2 * batch] + early[batch : 2 * batch],
        near[2 * batch :],
        early[2 * batch :],
        late,
    ]
    arrivals = [new for new in arrivals if new]
    spectra, olds, carried = [], [], None
    for new in arrivals:
        last = new is arrivals[-1]
        made = absorb(
            [blocks[step] for step in new],
            new,
            spectra,
            list(olds),
            carried,
            tile_order,
            lag_order,
            count,
            outer,
            inner,
            last,
        )
        if not last:
            carried, fresh = made
            spectra.append(fresh)
            olds.append(new)
    together = [
        [place * ways + way * inner + core for place in turns(count) for way in reversed(range(outer))]
        for core in range(inner)
    ]
    owned = lax.all_to_all(
        made, ("seq", "ch"), split_axis=0, concat_axis=0, axis_index_groups=together, tiled=True
    )
    squares = owned[:, :, groups * rows :]
    if inner == 2:
        pairs = [(place, place ^ 1) for place in range(ways)]
        squares = squares + lax.ppermute(squares, "ch", pairs)
    total = jnp.sum(squares, axis=(0, 1))
    lags = gather(owned, count, groups, rows, inner)
    entries = ways * count * groups * count * rows
    factor = target_ratio * math.sqrt(entries) / jnp.sqrt(total[:1] + epsilon)
    return lags * factor


def solution(mesh):
    return jax.shard_map(
        shards,
        mesh=mesh,
        in_specs=(P("seq", "ch"), P("seq", "ch"), P(), P()),
        out_specs=P("ch", "seq"),
        check_vma=False,
    )
```
